512 devices in a mesh: tm: 32 (over y, x, core), head: 16 (over z).
Axes of the slice: x: 4, y: 4, z: 16, core: 2. Of those that a mesh axis runs over, the one named last changes fastest.
Arguments:
- frame_inputs: bfloat16 [32768, 4096], P('tm', 'head'), may hold values from -6 to 6
- write_map: bfloat16 [32768, 128], P('tm'), may hold values from -0.29882812 to 0.29882812
- read_map: bfloat16 [32768, 128], P('tm'), may hold values from -0.29882812 to 0.29882812
- log_decay: float32 [64, 32768], P('head', 'tm'), may hold values from -1 to 0, as said below
- out_weight: bfloat16 [2048, 4096], P(None, 'head'), may hold values from -0.09375 to 0.09375
- caption_grad: float32 [1024, 2048], P('tm', 'head'), may hold values from -150 to 150
- caption_start: int32 [1024], P('tm'), may hold values from 0 to 32767, as said below
- caption_end: int32 [1024], P('tm'), may hold values from 1 to 32768, as said below
Outputs:
- grad_inputs: bfloat16 [32768, 4096], P('tm', 'head')
- grad_write: float32 [32768, 128], P(('tm', 'head'))
- grad_read: float32 [32768, 128], P(('tm', 'head'))
- grad_out_weight: float32 [2048, 4096], P('tm', 'head')
The draws below stay inside these ranges and needn't reach their ends.
Inputs may be any that keep to these rules, and one draw needn't show every extreme that they name: `caption_start`: caption k belongs to index k // 32 of tm: its segment starts in that index's frames, at 1024 * (k // 32) or later and before 1024 * (k // 32 + 1). `caption_end`: each segment has at most 200 frames and at least one; some caption's segment has exactly 200. Segments of different captions may share frames, and a segment may end in the following index's frames. `log_decay`: every entry is negative.
All inputs are finite; a program needn't handle non-finite values.
Results may differ from the reference program's by a relative error of at most 0.022.
Values may be sent and summed in bfloat16 or wider, within the bound.
A program may use at most 64 MiB of HBM per device.

```python
import jax
import jax.numpy as jnp
from jax import lax

D = 2048
RECURRENT_UNITS = 64
P_SIZE = 64
N = 128
BLOCK = 256
SEG_MOST = 200
FR_DEV = 1024
CAP_DEV = 32
CLIP_COUNT_ALL = 32768
CAPTIONS = 1024
N_TM = 32


def draw_log_decay(key, part):
    source_series = jax.random.split(jax.random.fold_in(key, 11), 6)
    fast_share = 0.5
    visible_motif = jnp.exp(jax.random.uniform(source_series[4], (RECURRENT_UNITS, CLIP_COUNT_ALL), minval=-0.6931, maxval=0.6931))
    fast_head = jax.random.bernoulli(source_series[0], fast_share, (RECURRENT_UNITS, 1))
    fast_rate = jax.random.uniform(source_series[1], (RECURRENT_UNITS, 1), minval=1.0 / 50.0, maxval=1.0 / 30.0)
    slow_rate = jax.random.uniform(source_series[2], (RECURRENT_UNITS, 1), minval=0.2, maxval=0.6) / CLIP_COUNT_ALL
    fading_rate = jnp.where(fast_head, fast_rate, slow_rate)
    spike_onset_slot = jax.random.randint(source_series[3], (2,), 0, CLIP_COUNT_ALL)
    clip_timestep = jnp.arange(CLIP_COUNT_ALL)[None, :]
    within_spike_flags = (clip_timestep == spike_onset_slot[0]) | (clip_timestep == spike_onset_slot[1])
    spike_cost_term = jax.random.uniform(source_series[5], (RECURRENT_UNITS, 1), minval=0.2, maxval=0.4)
    scalar_element = jnp.where(within_spike_flags, jnp.log(1.0 - spike_cost_term), 0.0) - fading_rate * visible_motif
    return scalar_element.astype(jnp.float32)


def caption_bounds(key):
    source_series = jax.random.split(jax.random.fold_in(key, 23), 3)
    lengths = jax.random.randint(source_series[0], (CAPTIONS,), SEG_MOST // 4, SEG_MOST + 1)
    longest = jax.random.randint(source_series[1], (), 0, CAP_DEV - 1) * 0 + jax.random.randint(source_series[1], (), 0, N_TM) * CAP_DEV
    caption_id = jnp.arange(CAPTIONS)
    lengths = jnp.where(caption_id == longest, SEG_MOST, lengths)
    owner_dev = caption_id // CAP_DEV
    offset = jax.random.randint(source_series[2], (CAPTIONS,), 0, FR_DEV)
    spill_offset = FR_DEV - jnp.maximum(lengths // 2, 1)
    offset = jnp.where(caption_id % CAP_DEV == CAP_DEV - 1, spill_offset, offset)
    starts = jnp.minimum(owner_dev * FR_DEV + offset, CLIP_COUNT_ALL - lengths)
    return (starts.astype(jnp.int32), (starts + lengths).astype(jnp.int32))


def draw_caption_start(key, part):
    return caption_bounds(key)[0]


def draw_caption_end(key, part):
    return caption_bounds(key)[1]


def block_scale(own_key, extent, cuts, low, high):
    loudness = 1.0
    for dim, shards_of in cuts:
        heights = jax.random.uniform(jax.random.fold_in(jax.random.fold_in(own_key, 6), dim), (shards_of,), jnp.float32, low / len(cuts), high / len(cuts))
        loudness = loudness * jnp.repeat(jnp.exp(heights), extent[dim] // shards_of).reshape((-1,) + (1,) * (len(extent) - 1 - dim))
    return loudness


def gaussian(own_key, shape, scale, bound, shards=(), held_as=jnp.bfloat16):
    values = scale * jax.random.normal(own_key, shape, jnp.float32)
    if shards:
        values = values * block_scale(own_key, shape, shards, -0.22, 0.18)
    return jnp.clip(values, -bound, bound).astype(held_as)


def setup_inputs(seed: int = 0) -> dict:
    key_list = jax.random.split(jax.random.key(seed), 9)
    frame_inputs = gaussian(key_list[0], (CLIP_COUNT_ALL, RECURRENT_UNITS * P_SIZE), 1.0, 6.0, ((0, 32), (1, 16)))
    write_map = gaussian(key_list[1], (CLIP_COUNT_ALL, N), 0.05, 0.29882812, ((0, 32),))
    read_map = gaussian(key_list[2], (CLIP_COUNT_ALL, N), 0.05, 0.29882812, ((0, 32),))
    log_decay = draw_log_decay(jax.random.fold_in(key_list[8], 71), 0)
    out_weight = gaussian(key_list[4], (D, RECURRENT_UNITS * P_SIZE), (RECURRENT_UNITS * P_SIZE) ** -0.5, 0.09375, ((1, 16),))
    caption_grad = gaussian(key_list[5], (CAPTIONS, D), 25.0, 150.0, ((0, 32), (1, 16)), jnp.float32)
    caption_start = draw_caption_start(jax.random.fold_in(key_list[8], 71), 0)
    caption_end = draw_caption_end(jax.random.fold_in(key_list[8], 71), 0)
    return dict(frame_inputs=frame_inputs, write_map=write_map, read_map=read_map, log_decay=log_decay, out_weight=out_weight, caption_grad=caption_grad, caption_start=caption_start, caption_end=caption_end)


HIGH = lax.Precision.HIGHEST


def narrow(scalar_element):
    return lax.optimization_barrier(scalar_element.astype(jnp.bfloat16)).astype(jnp.float32)


def block_terms(inputs32, write32, read32, grads32, running):
    causal = jnp.arange(BLOCK)[:, None] >= jnp.arange(BLOCK)[None, :]
    log_gap = running[:, :, None] - running[:, None, :]
    decay_mat = jnp.where(causal[None], jnp.exp(jnp.where(causal[None], log_gap, 0.0)), 0.0)
    intersection = jnp.einsum('tn,sn->ts', read32, write32)
    scores = narrow(intersection[None] * decay_mat)
    pairing = jnp.einsum('thp,shp->hts', inputs32, grads32)
    cross_terms = narrow(decay_mat * jnp.swapaxes(pairing, 1, 2))
    return scores, cross_terms


def forward_step(carry_state, pieces):
    inputs, write_rows, read_rows, grads, running = pieces
    inputs32 = inputs.astype(jnp.float32)
    write32 = write_rows.astype(jnp.float32)
    read32 = read_rows.astype(jnp.float32)
    grads32 = grads.astype(jnp.float32)
    scores, cross_terms = block_terms(inputs32, write32, read32, grads32, running)
    totals = running[:, -1]
    growth = jnp.exp(running)
    entry_b = narrow(carry_state)
    out_intra = jnp.einsum('hts,shp->thp', scores, inputs32)
    out_inter = jnp.einsum('tn,hnp->thp', read32, entry_b) * jnp.swapaxes(growth, 0, 1)[:, :, None]
    layer_out = (out_intra + out_inter).astype(jnp.bfloat16)
    read_intra = jnp.einsum('hts,sn->tn', cross_terms, write32)
    read_inter = jnp.sum(jnp.einsum('hnp,thp->htn', entry_b, grads32) * growth[:, :, None], axis=0)
    weighted_write = narrow(jnp.exp(totals[:, None] - running)[:, :, None] * write32[None])
    block_state = jnp.einsum('hsn,shp->hnp', weighted_write, inputs32)
    carry_state = jnp.exp(totals)[:, None, None] * carry_state + block_state
    return carry_state, (layer_out, read_intra + read_inter)


def reverse_step(carry_adj, pieces):
    inputs, write_rows, read_rows, grads, running = pieces
    inputs32 = inputs.astype(jnp.float32)
    write32 = write_rows.astype(jnp.float32)
    read32 = read_rows.astype(jnp.float32)
    grads32 = grads.astype(jnp.float32)
    scores, cross_terms = block_terms(inputs32, write32, read32, grads32, running)
    totals = running[:, -1]
    fading = jnp.exp(totals[:, None] - running)
    exit_b = narrow(carry_adj)
    in_intra = jnp.einsum('hst,shp->thp', scores, grads32)
    in_inter = jnp.einsum('tn,hnp->thp', write32, exit_b) * jnp.swapaxes(fading, 0, 1)[:, :, None]
    grad_inputs = (in_intra + in_inter).astype(jnp.bfloat16)
    write_intra = jnp.einsum('hst,sn->tn', cross_terms, read32)
    write_inter = jnp.sum(jnp.einsum('hnp,thp->htn', exit_b, inputs32) * fading[:, :, None], axis=0)
    weighted_read = narrow(jnp.exp(running)[:, :, None] * read32[None])
    block_adj = jnp.einsum('hsn,shp->hnp', weighted_read, grads32)
    carry_adj = jnp.exp(totals)[:, None, None] * carry_adj + block_adj
    return carry_adj, (grad_inputs, write_intra + write_inter)


def reference(frame_inputs, write_map, read_map, log_decay, out_weight, caption_grad, caption_start, caption_end):
    frames_all = frame_inputs.shape[0]
    head_count = log_decay.shape[0]
    head_size = frame_inputs.shape[1] // head_count
    seg_len = (caption_end - caption_start).astype(jnp.float32)
    frame_ids = jnp.arange(frames_all).astype(jnp.int32)[:, None]
    inside = (frame_ids >= caption_start[None, :]) & (frame_ids < caption_end[None, :])
    weights = jnp.where(inside, 1.0 / seg_len[None, :], 0.0)
    frame_grad = jnp.dot(weights, caption_grad, precision=HIGH).astype(jnp.bfloat16)
    grad_y = jnp.dot(frame_grad, out_weight, preferred_element_type=jnp.float32).astype(jnp.bfloat16)
    block_total = frames_all // BLOCK
    inputs = frame_inputs.reshape(block_total, BLOCK, head_count, head_size)
    grads = grad_y.reshape(block_total, BLOCK, head_count, head_size)
    write_rows = write_map.reshape(block_total, BLOCK, N)
    read_rows = read_map.reshape(block_total, BLOCK, N)
    running = jnp.swapaxes(jnp.cumsum(log_decay.reshape(head_count, block_total, BLOCK), axis=2), 0, 1)
    start_state = jnp.zeros((head_count, N, head_size), jnp.float32)
    pieces = (inputs, write_rows, read_rows, grads, running)
    _, (out_blocks, read_blocks) = lax.scan(forward_step, start_state, pieces)
    _, (input_blocks, write_blocks) = lax.scan(reverse_step, start_state, pieces, reverse=True)
    layer_out = out_blocks.reshape(frames_all, head_count * head_size)
    grad_inputs = input_blocks.reshape(frames_all, head_count * head_size)
    grad_write = write_blocks.reshape(frames_all, N)
    grad_read = read_blocks.reshape(frames_all, N)
    grad_out_weight = lax.dot_general(frame_grad, layer_out, (((0,), (0,)), ((), ())), preferred_element_type=jnp.float32)
    return (grad_inputs, grad_write, grad_read, grad_out_weight)
```

```python
import jax
import jax.numpy as jnp
from jax import lax
from jax.experimental import pallas as pl
from jax.experimental.pallas import tpu as pltpu
from jax.sharding import PartitionSpec as P

BLOCK = 256
F32 = jnp.float32
BF16 = jnp.bfloat16
MESH = pl.DeviceIdType.MESH
HIGH = lax.Precision.HIGHEST
N_TM = 32
N_HEAD = 16
CHIPS = N_TM // 2
NB = 4
NH = 4
CAP = 32


def mm(a, b):
    return lax.dot_general(a, b, (((1,), (0,)), ((), ())), preferred_element_type=F32)


def mm_nt(a, b):
    return lax.dot_general(a, b, (((1,), (1,)), ((), ())), preferred_element_type=F32)


def mm_tn(a, b):
    return lax.dot_general(a, b, (((0,), (0,)), ((), ())), preferred_element_type=F32)


def block_rows(b, size=BLOCK):
    return pl.ds(pl.multiple_of(b * size, size), size)


def kernel(
    x_ref, write_ref, read_ref, decay_ref, weight_ref, cap_ref, start_ref, end_ref,
    gi_ref, gw_ref, gr_ref, gow_ref,
    cgat, cols, meta, meta_prev, zown, zprev, zst, mask, hm,
    ld8, rowrun, growx, fadex, totx, xf, gg, gy, sblk, ablk, decay, scores, cross,
    out_acc, in_acc, wr_acc, entry, leave,
    dev, dev_b, pair_s, pair_a, adj, adj_b, lg, lg_pair, lgt, st_t, ad_t, tot_s, tot_a, ent, ext,
    lay, ppart, pprev, plb, rs_r, rs_w, rr, rw,
    c_s, c_r, cols_s, cols_r, one_s, one_r, lg_s, lg_r, t_s, t_r, a_s, a_r, pl_s, pl_r, rr_s, rr_r, rw_s, rw_r,
):
    me = lax.axis_index("tm")
    z = lax.axis_index("head")
    chip = me // 2
    core = me % 2
    pair = me + 1 - 2 * core
    nxt = (me + 1) % N_TM
    prv = (me + N_TM - 1) % N_TM

    def send(src, dst, s, r, **where):
        return pltpu.make_async_remote_copy(
            src_ref=src, dst_ref=dst, send_sem=s, recv_sem=r, device_id=where, device_id_type=MESH
        )

    barrier = pltpu.get_barrier_semaphore()

    def hail_tm(d, carry):
        pl.semaphore_signal(barrier, inc=1, device_id={"tm": (me + d) % N_TM}, device_id_type=MESH)
        return carry

    def hail_head(d, carry):
        pl.semaphore_signal(barrier, inc=1, device_id={"head": (z + d) % N_HEAD}, device_id_type=MESH)
        return carry

    lax.fori_loop(1, N_TM, hail_tm, 0)
    lax.fori_loop(1, N_HEAD, hail_head, 0)

    cgat[z] = cap_ref[...].astype(BF16)
    spread = (
        lax.broadcasted_iota(jnp.int32, (CAP, 128), 1) % CAP
        == lax.broadcasted_iota(jnp.int32, (CAP, 128), 0)
    ).astype(F32)
    start_f = start_ref[...].astype(F32)
    end_f = end_ref[...].astype(F32)
    start_row = jnp.dot(jnp.broadcast_to(start_f, (8, CAP)), spread, precision=HIGH, preferred_element_type=F32)
    end_row = jnp.dot(jnp.broadcast_to(end_f, (8, CAP)), spread, precision=HIGH, preferred_element_type=F32)
    meta[0] = start_row
    meta[1] = end_row
    eye = lax.broadcasted_iota(jnp.int32, (CAP, CAP), 0) == lax.broadcasted_iota(jnp.int32, (CAP, CAP), 1)
    inv_len = jnp.sum(jnp.where(eye, 1.0 / jnp.maximum(end_f - start_f, 1.0), 0.0), axis=1, keepdims=True)

    pl.semaphore_wait(barrier, N_TM - 1 + N_HEAD - 1)

    for d in (8, 7, 9, 6, 10, 5, 11, 4, 12, 3, 13, 2, 14, 1, 15):
        send(cgat.at[z], cgat.at[z], c_s.at[d], c_r.at[z], head=(z + d) % N_HEAD).start()
    meta_copy = send(meta, meta_prev, one_s.at[0], one_r.at[0], tm=nxt)
    meta_copy.start()

    lane_head = lax.broadcasted_iota(jnp.int32, (BLOCK, BLOCK), 1) // 64
    row_id = lax.broadcasted_iota(jnp.int32, (BLOCK, BLOCK), 0)
    col_id = lax.broadcasted_iota(jnp.int32, (BLOCK, BLOCK), 1)
    for h in range(NH):
        hm[h] = (lane_head == h).astype(F32).astype(BF16)
    tri = (row_id <= col_id).astype(F32)
    ld8[...] = jnp.zeros_like(ld8)
    ld8[0:4, :] = decay_ref[...]

    def local_state(b, carry):
        rows = block_rows(b)
        run = jnp.dot(ld8[:, rows], tri, precision=HIGH, preferred_element_type=F32)
        rowrun[b] = run
        col = run.T
        runx = jnp.where(
            lane_head < 2,
            jnp.where(lane_head < 1, col[:, 0:1], col[:, 1:2]),
            jnp.where(lane_head < 3, col[:, 2:3], col[:, 3:4]),
        )
        total = runx[BLOCK - 1 : BLOCK, :]
        growx[b] = jnp.exp(runx)
        fade = jnp.exp(total - runx)
        fadex[b] = fade
        totx[b] = jnp.broadcast_to(total, (8, BLOCK))
        faded = (x_ref[rows, :].astype(F32) * fade).astype(BF16)
        xf[b] = faded
        sblk[b] = mm_tn(write_ref[rows, :], faded)
        return carry

    lax.fori_loop(0, NB, local_state, 0)

    state = sblk[0]
    for b in range(1, NB):
        state = jnp.exp(totx[b, 0:1, :]) * state + sblk[b]
    log_all = totx[0] + totx[1] + totx[2] + totx[3]
    for half in range(2):
        cut = slice(128 * half, 128 * half + 128)
        dev[half] = state[:, cut]
        dev_b[half] = state[:, cut].astype(BF16)
        lg[half] = log_all[:, cut]
    state_copy = send(dev_b, pair_s, one_s.at[1], one_r.at[1], tm=pair)
    state_copy.start()
    lg_copy = send(lg, lg_pair, one_s.at[2], one_r.at[2], tm=pair)
    lg_copy.start()

    def local_scores(b, carry):
        rows = block_rows(b)
        both = mm_nt(read_ref[rows, :], write_ref[rows, :])
        run = rowrun[b]
        col = run.T
        xb = x_ref[rows, :]
        out = jnp.zeros((BLOCK, BLOCK), F32)
        for h in range(NH):
            gap = col[:, h : h + 1] - run[h : h + 1, :]
            dec = jnp.exp(jnp.where(row_id >= col_id, gap, -jnp.inf))
            decay[b * NH + h] = dec
            sc = (both * dec).astype(BF16)
            scores[b * NH + h] = sc
            out += mm(sc, xb * hm[h])
        out_acc[b] = out
        return carry

    lax.fori_loop(0, 2, local_scores, 0)

    state_copy.wait_recv()
    lg_copy.wait_recv()
    first = core == 0
    log0 = [jnp.where(first, lg[h], lg_pair[h])[0:1, :] for h in range(2)]
    log1 = [jnp.where(first, lg_pair[h], lg[h])[0:1, :] for h in range(2)]

    mine = dev[core]
    other = pair_s[core].astype(F32)
    s0 = jnp.where(first, mine, other)
    s1 = jnp.where(first, other, mine)
    l0 = jnp.where(first, log0[0], log0[1])
    l1 = jnp.where(first, log1[0], log1[1])
    tot_s[...] = (s1 + jnp.exp(l1) * s0).astype(BF16)
    lgt[chip] = jnp.broadcast_to(l0 + l1, (8, 128))

    def send_log(d, carry):
        to = (chip + d) % CHIPS
        send(lgt.at[chip], lgt.at[chip], lg_s.at[to], lg_r.at[chip], tm=to * 2 + core).start()
        return carry

    def send_state(to, carry):
        send(tot_s, st_t.at[chip], t_s.at[to], t_r.at[chip], tm=to * 2 + core).start()
        return carry

    lax.fori_loop(1, CHIPS, send_log, 0)
    lax.fori_loop(chip + 1, CHIPS, send_state, 0)
    lax.fori_loop(2, NB, local_scores, 0)

    proj = mm(cgat[z], weight_ref[block_rows(z, 128), :])
    for d in (1, 15, 2, 14, 3, 13, 4, 12, 5, 11, 6, 10, 7, 9, 8):
        frm = (z + d) % N_HEAD
        send(cgat.at[frm], cgat.at[frm], c_s.at[d], c_r.at[frm], head=frm).wait_recv()
        proj += mm(cgat[frm], weight_ref[block_rows(frm, 128), :])
    proj = proj * inv_len
    zown[...] = proj
    z_copy = send(zown, zprev, one_s.at[3], one_r.at[3], tm=nxt)
    z_copy.start()

    cols[me] = cgat[chip]

    def send_cols(d, carry):
        to = (me + d) % N_TM
        send(cgat.at[to // 2], cols.at[me], cols_s.at[to], cols_r.at[me], tm=to).start()
        return carry

    lax.fori_loop(1, N_TM, send_cols, 0)

    meta_copy.wait_recv()
    lane = lax.broadcasted_iota(jnp.int32, (BLOCK, 128), 1)
    frame = lax.broadcasted_iota(jnp.int32, (BLOCK, 128), 0)
    seg_start = jnp.where(lane[0:8] < 64, meta[0], meta_prev[0])[0:1, :]
    seg_end = jnp.where(lane[0:8] < 64, meta[1], meta_prev[1])[0:1, :]

    def cover(b, carry):
        t = (frame + (me * (NB * BLOCK) + b * BLOCK)).astype(F32)
        inside = jnp.where(t >= seg_start, jnp.where(t < seg_end, 1.0, 0.0), 0.0)
        mask[block_rows(b), :] = inside.astype(BF16)
        return carry

    lax.fori_loop(0, NB, cover, 0)

    def await_log(d, carry):
        frm = (chip + d) % CHIPS
        send(lgt.at[frm], lgt.at[frm], lg_s.at[frm], lg_r.at[frm], tm=frm * 2 + core).wait_recv()
        return carry

    lax.fori_loop(1, CHIPS, await_log, 0)

    def take_state(m, acc):
        send(tot_s, st_t.at[m], t_s.at[m], t_r.at[m], tm=m * 2 + core).wait_recv()
        return jnp.exp(lgt[m][0:1, :]) * acc + st_t[m].astype(F32)

    ent[core] = lax.fori_loop(0, chip, take_state, jnp.zeros((128, 128), F32))
    ent_copy = send(ent.at[core], ent.at[core], one_s.at[4], one_r.at[4 + core], tm=pair)
    ent_copy.start()

    hi = proj.astype(BF16)
    zst[0:32, :] = hi
    zst[32:64, :] = (proj - hi.astype(F32)).astype(BF16)
    z_copy.wait_recv()
    before = zprev[...]
    hi = before.astype(BF16)
    zst[64:96, :] = hi
    zst[96:128, :] = (before - hi.astype(F32)).astype(BF16)

    def local_adjoint(b, carry):
        rows = block_rows(b)
        g = mm(mask[rows, :], zst[...]).astype(BF16)
        gy[b] = g
        grown = (g.astype(F32) * growx[b]).astype(BF16)
        gg[b] = grown
        ablk[b] = mm_tn(read_ref[rows, :], grown)
        return carry

    lax.fori_loop(0, NB, local_adjoint, 0)
    back = ablk[NB - 1]
    for b in range(NB - 2, -1, -1):
        back = jnp.exp(totx[b, 0:1, :]) * back + ablk[b]
    for half in range(2):
        cut = slice(128 * half, 128 * half + 128)
        adj[half] = back[:, cut]
        adj_b[half] = back[:, cut].astype(BF16)
    adj_copy = send(adj_b, pair_a, one_s.at[6], one_r.at[6], tm=pair)
    adj_copy.start()

    send(ent.at[core], ent.at[1 - core], one_s.at[4], one_r.at[5 - core], tm=pair).wait_recv()
    halves = []
    for half in range(2):
        came = ent[half]
        halves.append(jnp.where(first, came, jnp.exp(log0[half]) * came + pair_s[half].astype(F32)))
    carry_state = jnp.concatenate(halves, axis=1)
    for b in range(NB):
        entry[b] = carry_state.astype(BF16)
        if b < NB - 1:
            carry_state = jnp.exp(totx[b, 0:1, :]) * carry_state + sblk[b]

    adj_copy.wait_recv()
    mine = adj[core]
    other = pair_a[core].astype(F32)
    a0 = jnp.where(first, mine, other)
    a1 = jnp.where(first, other, mine)
    tot_a[...] = (a0 + jnp.exp(l0) * a1).astype(BF16)

    def send_adjoint(to, carry):
        send(tot_a, ad_t.at[chip], a_s.at[to], a_r.at[chip], tm=to * 2 + core).start()
        return carry

    lax.fori_loop(0, chip, send_adjoint, 0)

    def pooled(b, acc):
        rows = block_rows(b)
        y = (out_acc[b] + growx[b] * mm(read_ref[rows, :], entry[b])).astype(BF16)
        lay[rows, :] = y
        return acc + mm_tn(mask[rows, :], y)

    pool = lax.fori_loop(0, NB, pooled, jnp.zeros((128, BLOCK), F32))
    ppart[...] = pool[64:96, :]
    p_copy = send(ppart, pprev, one_s.at[7], one_r.at[7], tm=prv)
    p_copy.start()

    def send_part(buf, into, s, r, b):
        for k in range(4):
            to = b * 4 + k

            @pl.when(to != z)
            def _():
                send(buf.at[to], into.at[z], s.at[to], r.at[z], head=to).start()

    def local_cross(i, carry):
        b = (i + z // 4 + 2) % NB
        rows = block_rows(b)
        g = gy[b]
        xb = x_ref[rows, :]
        both = jnp.zeros((BLOCK, BLOCK), F32)
        into = jnp.zeros((BLOCK, BLOCK), F32)
        for h in range(NH):
            gh = g * hm[h]
            both += decay[b * NH + h] * mm_nt(gh, xb)
            into += mm_tn(scores[b * NH + h], gh)
        in_acc[b] = into
        both = both.astype(BF16)
        part = mm(both, write_ref[rows, :]) + mm_nt(gg[b], entry[b])
        for k in range(4):
            rs_r[b * 4 + k] = part[64 * k : 64 * k + 64, :].astype(BF16)
        send_part(rs_r, rr, rr_s, rr_r, b)
        wr_acc[b] = mm_tn(both, read_ref[rows, :])
        return carry

    lax.fori_loop(0, NB, local_cross, 0)

    p_copy.wait_recv()
    plb[me] = ((pool[0:32, :] + pprev[...]) * inv_len).astype(BF16)

    def send_pool(d, carry):
        to = (me + d) % N_TM
        send(plb.at[me], plb.at[me], pl_s.at[to], pl_r.at[me], tm=to).start()
        return carry

    def take_adjoint(i, acc):
        m = CHIPS - 1 - i
        send(tot_a, ad_t.at[m], a_s.at[m], a_r.at[m], tm=m * 2 + core).wait_recv()
        return jnp.exp(lgt[m][0:1, :]) * acc + ad_t[m].astype(F32)

    ext[core] = lax.fori_loop(0, CHIPS - 1 - chip, take_adjoint, jnp.zeros((128, 128), F32))
    ext_copy = send(ext.at[core], ext.at[core], one_s.at[8], one_r.at[8 + core], tm=pair)
    ext_copy.start()
    lax.fori_loop(1, N_TM, send_pool, 0)
    send(ext.at[core], ext.at[1 - core], one_s.at[8], one_r.at[9 - core], tm=pair).wait_recv()
    halves = []
    for half in range(2):
        came = ext[half]
        halves.append(jnp.where(first, jnp.exp(log1[half]) * came + pair_a[half].astype(F32), came))
    carry_adj = jnp.concatenate(halves, axis=1)
    for b in range(NB - 1, -1, -1):
        leave[b] = carry_adj.astype(BF16)
        if b > 0:
            carry_adj = jnp.exp(totx[b, 0:1, :]) * carry_adj + ablk[b]

    def late_write(i, carry):
        b = (i + z // 4 + 2) % NB
        part = wr_acc[b] + mm_nt(xf[b], leave[b])
        for k in range(4):
            rs_w[b * 4 + k] = part[64 * k : 64 * k + 64, :].astype(BF16)
        send_part(rs_w, rw, rw_s, rw_r, b)
        return carry

    lax.fori_loop(0, NB, late_write, 0)

    def late_inputs(b, carry):
        rows = block_rows(b)
        gi_ref[rows, :] = (in_acc[b] + fadex[b] * mm(write_ref[rows, :], leave[b])).astype(BF16)
        return carry

    lax.fori_loop(0, NB, late_inputs, 0)

    def await_pool(d, carry):
        frm = (me + d) % N_TM
        send(cgat.at[0], cols.at[frm], cols_s.at[frm], cols_r.at[frm], tm=frm).wait_recv()
        send(plb.at[frm], plb.at[frm], pl_s.at[frm], pl_r.at[frm], tm=frm).wait_recv()
        return carry

    lax.fori_loop(1, N_TM, await_pool, 0)
    weight_grad = mm_tn(cols[...].reshape(N_TM * CAP, 128), plb[...].reshape(N_TM * CAP, BLOCK))
    gow_ref[...] = jnp.where(first, weight_grad[0:64, :], weight_grad[64:128, :])

    def take(buf, into, s, r):
        def step(d, acc):
            frm = (z + d) % N_HEAD
            send(buf.at[frm], into.at[frm], s.at[frm], r.at[frm], head=frm).wait_recv()
            return acc + into[frm].astype(F32)

        return lax.fori_loop(1, N_HEAD, step, buf[z].astype(F32))

    gr_ref[...] = take(rs_r, rr, rr_s, rr_r)
    gw_ref[...] = take(rs_w, rw, rw_s, rw_r)

    for d in range(1, N_HEAD):
        send(cgat.at[z], cgat.at[z], c_s.at[d], c_r.at[z], head=(z + d) % N_HEAD).wait_send()
    for copy in (meta_copy, state_copy, lg_copy, z_copy, ent_copy, adj_copy, p_copy, ext_copy):
        copy.wait_send()

    def sent_tm(d, carry):
        to = (me + d) % N_TM
        send(cgat.at[0], cols.at[me], cols_s.at[to], cols_r.at[me], tm=to).wait_send()
        send(plb.at[me], plb.at[me], pl_s.at[to], pl_r.at[me], tm=to).wait_send()
        return carry

    def sent_log(d, carry):
        to = (chip + d) % CHIPS
        send(lgt.at[chip], lgt.at[chip], lg_s.at[to], lg_r.at[chip], tm=to * 2 + core).wait_send()
        return carry

    def sent_state(to, carry):
        send(tot_s, st_t.at[chip], t_s.at[to], t_r.at[chip], tm=to * 2 + core).wait_send()
        return carry

    def sent_adjoint(to, carry):
        send(tot_a, ad_t.at[chip], a_s.at[to], a_r.at[chip], tm=to * 2 + core).wait_send()
        return carry

    def sent_head(d, carry):
        to = (z + d) % N_HEAD
        send(rs_r.at[to], rr.at[z], rr_s.at[to], rr_r.at[z], head=to).wait_send()
        send(rs_w.at[to], rw.at[z], rw_s.at[to], rw_r.at[z], head=to).wait_send()
        return carry

    lax.fori_loop(1, N_TM, sent_tm, 0)
    lax.fori_loop(1, CHIPS, sent_log, 0)
    lax.fori_loop(chip + 1, CHIPS, sent_state, 0)
    lax.fori_loop(0, chip, sent_adjoint, 0)
    lax.fori_loop(1, N_HEAD, sent_head, 0)


def body(frame_inputs, write_map, read_map, log_decay, out_weight, caption_grad, caption_start, caption_end):
    frames, width = frame_inputs.shape
    V = pltpu.VMEM
    DMA = pltpu.SemaphoreType.DMA
    state = (2, 128, 128)
    tile = (BLOCK, BLOCK)
    scratch = [
        V((N_HEAD, CAP, 128), BF16),
        V((N_TM, CAP, 128), BF16),
        V((2, 8, 128), F32),
        V((2, 8, 128), F32),
        V((CAP, BLOCK), F32),
        V((CAP, BLOCK), F32),
        V((128, BLOCK), BF16),
        V((frames, 128), BF16),
        V((NH, *tile), BF16),
        V((8, frames), F32),
        V((NB, 8, BLOCK), F32),
        V((NB, *tile), F32),
        V((NB, *tile), F32),
        V((NB, 8, BLOCK), F32),
        V((NB, *tile), BF16),
        V((NB, *tile), BF16),
        V((NB, *tile), BF16),
        V((NB, 128, BLOCK), F32),
        V((NB, 128, BLOCK), F32),
        V((NB * NH, *tile), F32),
        V((NB * NH, *tile), BF16),
        V((8, 128), BF16),
        V((NB, *tile), F32),
        V((NB, *tile), F32),
        V((NB, BLOCK, 128), F32),
        V((NB, 128, BLOCK), BF16),
        V((NB, 128, BLOCK), BF16),
        V(state, F32),
        V(state, BF16),
        V(state, BF16),
        V(state, BF16),
        V(state, F32),
        V(state, BF16),
        V((2, 8, 128), F32),
        V((2, 8, 128), F32),
        V((CHIPS, 8, 128), F32),
        V((CHIPS, 128, 128), BF16),
        V((CHIPS, 128, 128), BF16),
        V((128, 128), BF16),
        V((128, 128), BF16),
        V(state, F32),
        V(state, F32),
        V((frames, BLOCK), BF16),
        V((CAP, BLOCK), F32),
        V((CAP, BLOCK), F32),
        V((N_TM, CAP, BLOCK), BF16),
        V((N_HEAD, 64, 128), BF16),
        V((N_HEAD, 64, 128), BF16),
        V((N_HEAD, 64, 128), BF16),
        V((N_HEAD, 64, 128), BF16),
        DMA((N_HEAD,)),
        DMA((N_HEAD,)),
        DMA((N_TM,)),
        DMA((N_TM,)),
        DMA((10,)),
        DMA((10,)),
        DMA((CHIPS,)),
        DMA((CHIPS,)),
        DMA((CHIPS,)),
        DMA((CHIPS,)),
        DMA((CHIPS,)),
        DMA((CHIPS,)),
        DMA((N_TM,)),
        DMA((N_TM,)),
        DMA((N_HEAD,)),
        DMA((N_HEAD,)),
        DMA((N_HEAD,)),
        DMA((N_HEAD,)),
    ]
    vmem = pl.BlockSpec(memory_space=pltpu.VMEM)
    return pl.pallas_call(
        kernel,
        out_shape=(
            jax.ShapeDtypeStruct((frames, width), BF16),
            jax.ShapeDtypeStruct((64, 128), F32),
            jax.ShapeDtypeStruct((64, 128), F32),
            jax.ShapeDtypeStruct((64, BLOCK), F32),
        ),
        in_specs=[vmem] * 8,
        out_specs=(vmem,) * 4,
        scratch_shapes=scratch,
        compiler_params=pltpu.CompilerParams(
            collective_id=0, has_side_effects=True, vmem_limit_bytes=48 * 1024 * 1024
        ),
    )(
        frame_inputs, write_map, read_map, log_decay, out_weight, caption_grad,
        caption_start.reshape(1, CAP), caption_end.reshape(1, CAP),
    )


def solution(mesh):
    in_specs = (
        P("tm", "head"),
        P("tm", None),
        P("tm", None),
        P("head", "tm"),
        P(None, "head"),
        P("tm", "head"),
        P("tm"),
        P("tm"),
    )
    out_specs = (P("tm", "head"), P(("tm", "head"), None), P(("tm", "head"), None), P("tm", "head"))
    return jax.shard_map(body, mesh=mesh, in_specs=in_specs, out_specs=out_specs, check_vma=False)
```

```python
import jax
import jax.numpy as jnp
from jax import lax
from jax.experimental import pallas as pl
from jax.experimental.pallas import tpu as pltpu
from jax.sharding import PartitionSpec as P

BLOCK = 256
F32 = jnp.float32
BF16 = jnp.bfloat16
MESH = pl.DeviceIdType.MESH
HIGH = lax.Precision.HIGHEST
N_TM = 32
N_HEAD = 16
CHIPS = N_TM // 2
NB = 4
NH = 4
CAP = 32


def mm(a, b):
    return lax.dot_general(a, b, (((1,), (0,)), ((), ())), preferred_element_type=F32)


def mm_nt(a, b):
    return lax.dot_general(a, b, (((1,), (1,)), ((), ())), preferred_element_type=F32)


def mm_tn(a, b):
    return lax.dot_general(a, b, (((0,), (0,)), ((), ())), preferred_element_type=F32)


def block_rows(b, size=BLOCK):
    return pl.ds(pl.multiple_of(b * size, size), size)


def kernel(
    x_hbm, write_hbm, read_hbm, decay_hbm, weight_hbm, cap_hbm, start_hbm, end_hbm,
    gi_ref, gw_ref, gr_ref, gow_ref,
    x_ref, write_ref, read_ref, decay_ref, weight_ref, cap_ref, start_ref, end_ref, in_s,
    cgat, cols, meta, meta_prev, zown, zprev, zst, mask, hm,
    ld8, rowrun, growx, fadex, totx, xf, gg, gy, sblk, ablk, decay, scores,
    out_acc, in_acc, wr_acc, entry, leave,
    dev, dev_b, pair_s, pair_a, adj, adj_b, lg, lg_pair, lgt, st_t, ad_t, tot_s, tot_a, ent, ext,
    ppart, pprev, plb, rs_r, rs_w, mid_r, mid_w, rr, rw, gi_vm,
    c_s, c_r, cols_s, cols_r, one_s, one_r, lg_s, lg_r, t_s, t_r, a_s, a_r, pl_s, pl_r, rr_s, rr_r, rw_s, rw_r, mid_r_s, mid_w_s,
):
    me = lax.axis_index("tm")
    z = lax.axis_index("head")
    chip = me // 2
    core = me % 2
    pair = me + 1 - 2 * core
    nxt = (me + 1) % N_TM
    prv = (me + N_TM - 1) % N_TM

    def send(src, dst, s, r, **where):
        return pltpu.make_async_remote_copy(
            src_ref=src, dst_ref=dst, send_sem=s, recv_sem=r, device_id=where, device_id_type=MESH
        )

    fetch = [
        pltpu.make_async_copy(src, dst, in_s.at[i])
        for i, (src, dst) in enumerate(
            (
                (cap_hbm, cap_ref),
                (start_hbm, start_ref),
                (end_hbm, end_ref),
                (decay_hbm, decay_ref),
                (x_hbm, x_ref),
                (write_hbm, write_ref),
                (read_hbm, read_ref),
                (weight_hbm, weight_ref),
            )
        )
    ]
    for copy in fetch:
        copy.start()
    barrier = pltpu.get_barrier_semaphore()

    def hail_tm(d, carry):
        pl.semaphore_signal(barrier, inc=1, device_id={"tm": (me + d) % N_TM}, device_id_type=MESH)
        return carry

    def hail_head(d, carry):
        pl.semaphore_signal(barrier, inc=1, device_id={"head": (z + d) % N_HEAD}, device_id_type=MESH)
        return carry

    lax.fori_loop(1, N_TM, hail_tm, 0)
    lax.fori_loop(1, N_HEAD, hail_head, 0)

    for copy in fetch[:3]:
        copy.wait()
    cgat[z] = cap_ref[...].astype(BF16)
    spread = (
        lax.broadcasted_iota(jnp.int32, (CAP, 128), 1) % CAP
        == lax.broadcasted_iota(jnp.int32, (CAP, 128), 0)
    ).astype(F32)
    start_f = start_ref[...].astype(F32)
    end_f = end_ref[...].astype(F32)
    start_row = jnp.dot(jnp.broadcast_to(start_f, (8, CAP)), spread, precision=HIGH, preferred_element_type=F32)
    end_row = jnp.dot(jnp.broadcast_to(end_f, (8, CAP)), spread, precision=HIGH, preferred_element_type=F32)
    meta[0] = start_row
    meta[1] = end_row
    eye = lax.broadcasted_iota(jnp.int32, (CAP, CAP), 0) == lax.broadcasted_iota(jnp.int32, (CAP, CAP), 1)
    inv_len = jnp.sum(jnp.where(eye, 1.0 / jnp.maximum(end_f - start_f, 1.0), 0.0), axis=1, keepdims=True)

    pl.semaphore_wait(barrier, N_TM - 1 + N_HEAD - 1)

    for d in (8, 7, 9, 6, 10, 5, 11, 4, 12, 3, 13, 2, 14, 1, 15):
        send(cgat.at[z], cgat.at[z], c_s.at[d], c_r.at[z], head=(z + d) % N_HEAD).start()
    meta_copy = send(meta, meta_prev, one_s.at[0], one_r.at[0], tm=nxt)
    meta_copy.start()

    lane_head = lax.broadcasted_iota(jnp.int32, (BLOCK, BLOCK), 1) // 64
    row_id = lax.broadcasted_iota(jnp.int32, (BLOCK, BLOCK), 0)
    col_id = lax.broadcasted_iota(jnp.int32, (BLOCK, BLOCK), 1)
    for h in range(NH):
        hm[h] = (lane_head == h).astype(F32).astype(BF16)
    tri = (row_id <= col_id).astype(F32)
    ld8[...] = jnp.zeros_like(ld8)
    fetch[3].wait()
    ld8[0:4, :] = decay_ref[...]
    fetch[4].wait()
    fetch[5].wait()

    def local_state(b, carry):
        rows = block_rows(b)
        run = jnp.dot(ld8[:, rows], tri, precision=HIGH, preferred_element_type=F32)
        rowrun[b] = run
        col = run.T
        runx = jnp.where(
            lane_head < 2,
            jnp.where(lane_head < 1, col[:, 0:1], col[:, 1:2]),
            jnp.where(lane_head < 3, col[:, 2:3], col[:, 3:4]),
        )
        total = runx[BLOCK - 1 : BLOCK, :]
        growx[b] = jnp.exp(runx)
        fade = jnp.exp(total - runx)
        fadex[b] = fade
        totx[b] = jnp.broadcast_to(total, (8, BLOCK))
        faded = (x_ref[rows, :].astype(F32) * fade).astype(BF16)
        xf[b] = faded
        sblk[b] = mm_tn(write_ref[rows, :], faded)
        return carry

    lax.fori_loop(0, NB, local_state, 0)

    state = sblk[0]
    for b in range(1, NB):
        state = jnp.exp(totx[b, 0:1, :]) * state + sblk[b]
    log_all = totx[0] + totx[1] + totx[2] + totx[3]
    for half in range(2):
        cut = slice(128 * half, 128 * half + 128)
        dev[half] = state[:, cut]
        dev_b[half] = state[:, cut].astype(BF16)
        lg[half] = log_all[:, cut]
    state_copy = send(dev_b, pair_s, one_s.at[1], one_r.at[1], tm=pair)
    state_copy.start()
    lg_copy = send(lg, lg_pair, one_s.at[2], one_r.at[2], tm=pair)
    lg_copy.start()

    fetch[6].wait()

    def local_scores(b, carry):
        rows = block_rows(b)
        both = mm_nt(read_ref[rows, :], write_ref[rows, :])
        run = rowrun[b]
        col = run.T
        xb = x_ref[rows, :]
        out = jnp.zeros((BLOCK, BLOCK), F32)
        for h in range(NH):
            gap = col[:, h : h + 1] - run[h : h + 1, :]
            dec = jnp.exp(jnp.where(row_id >= col_id, gap, -jnp.inf))
            decay[b * NH + h] = dec
            sc = (both * dec).astype(BF16)
            scores[b * NH + h] = sc
            out += mm(sc, xb * hm[h])
        out_acc[b] = out
        return carry

    lax.fori_loop(0, 2, local_scores, 0)

    state_copy.wait_recv()
    lg_copy.wait_recv()
    first = core == 0
    log0 = [jnp.where(first, lg[h], lg_pair[h])[0:1, :] for h in range(2)]
    log1 = [jnp.where(first, lg_pair[h], lg[h])[0:1, :] for h in range(2)]

    mine = dev[core]
    other = pair_s[core].astype(F32)
    s0 = jnp.where(first, mine, other)
    s1 = jnp.where(first, other, mine)
    l0 = jnp.where(first, log0[0], log0[1])
    l1 = jnp.where(first, log1[0], log1[1])
    tot_s[...] = (s1 + jnp.exp(l1) * s0).astype(BF16)
    lgt[chip] = jnp.broadcast_to(l0 + l1, (8, 128))

    def send_log(d, carry):
        to = (chip + d) % CHIPS
        send(lgt.at[chip], lgt.at[chip], lg_s.at[to], lg_r.at[chip], tm=to * 2 + core).start()
        return carry

    def send_state(to, carry):
        send(tot_s, st_t.at[chip], t_s.at[to], t_r.at[chip], tm=to * 2 + core).start()
        return carry

    lax.fori_loop(1, CHIPS, send_log, 0)
    lax.fori_loop(chip + 1, CHIPS, send_state, 0)
    lax.fori_loop(2, NB, local_scores, 0)

    fetch[7].wait()
    proj = mm(cgat[z], weight_ref[block_rows(z, 128), :])
    for d in (1, 15, 2, 14, 3, 13, 4, 12, 5, 11, 6, 10, 7, 9, 8):
        frm = (z + d) % N_HEAD
        send(cgat.at[frm], cgat.at[frm], c_s.at[d], c_r.at[frm], head=frm).wait_recv()
        proj += mm(cgat[frm], weight_ref[block_rows(frm, 128), :])
    proj = proj * inv_len
    zown[...] = proj
    z_copy = send(zown, zprev, one_s.at[3], one_r.at[3], tm=nxt)
    z_copy.start()

    cols[me] = cgat[chip]

    def send_cols(d, carry):
        to = (me + d) % N_TM
        send(cgat.at[to // 2], cols.at[me], cols_s.at[to], cols_r.at[me], tm=to).start()
        return carry

    lax.fori_loop(1, N_TM, send_cols, 0)

    meta_copy.wait_recv()
    lane = lax.broadcasted_iota(jnp.int32, (BLOCK, 128), 1)
    frame = lax.broadcasted_iota(jnp.int32, (BLOCK, 128), 0)
    seg_start = jnp.where(lane[0:8] < 64, meta[0], meta_prev[0])[0:1, :]
    seg_end = jnp.where(lane[0:8] < 64, meta[1], meta_prev[1])[0:1, :]

    def cover(b, carry):
        t = (frame + (me * (NB * BLOCK) + b * BLOCK)).astype(F32)
        inside = jnp.where(t >= seg_start, jnp.where(t < seg_end, 1.0, 0.0), 0.0)
        mask[block_rows(b), :] = inside.astype(BF16)
        return carry

    lax.fori_loop(0, NB, cover, 0)

    def await_log(d, carry):
        frm = (chip + d) % CHIPS
        send(lgt.at[frm], lgt.at[frm], lg_s.at[frm], lg_r.at[frm], tm=frm * 2 + core).wait_recv()
        return carry

    lax.fori_loop(1, CHIPS, await_log, 0)

    def take_state(m, acc):
        send(tot_s, st_t.at[m], t_s.at[m], t_r.at[m], tm=m * 2 + core).wait_recv()
        return jnp.exp(lgt[m][0:1, :]) * acc + st_t[m].astype(F32)

    ent[core] = lax.fori_loop(0, chip, take_state, jnp.zeros((128, 128), F32))
    ent_copy = send(ent.at[core], ent.at[core], one_s.at[4], one_r.at[4 + core], tm=pair)
    ent_copy.start()

    hi = proj.astype(BF16)
    zst[0:32, :] = hi
    zst[32:64, :] = (proj - hi.astype(F32)).astype(BF16)
    zst[64:128, :] = jnp.zeros((64, BLOCK), BF16)

    def local_adjoint(i, carry):
        b = NB - 1 - i
        rows = block_rows(b)
        g = mm(mask[rows, :], zst[...]).astype(BF16)
        gy[b] = g
        grown = (g.astype(F32) * growx[b]).astype(BF16)
        gg[b] = grown
        ablk[b] = mm_tn(read_ref[rows, :], grown)
        return carry

    lax.fori_loop(0, NB - 1, local_adjoint, 0)
    z_copy.wait_recv()
    before = zprev[...]
    hi = before.astype(BF16)
    zst[64:96, :] = hi
    zst[96:128, :] = (before - hi.astype(F32)).astype(BF16)
    lax.fori_loop(NB - 1, NB, local_adjoint, 0)
    back = ablk[NB - 1]
    for b in range(NB - 2, -1, -1):
        back = jnp.exp(totx[b, 0:1, :]) * back + ablk[b]
    for half in range(2):
        cut = slice(128 * half, 128 * half + 128)
        adj[half] = back[:, cut]
        adj_b[half] = back[:, cut].astype(BF16)
    adj_copy = send(adj_b, pair_a, one_s.at[6], one_r.at[6], tm=pair)
    adj_copy.start()

    send(ent.at[core], ent.at[1 - core], one_s.at[4], one_r.at[5 - core], tm=pair).wait_recv()
    halves = []
    for half in range(2):
        came = ent[half]
        halves.append(jnp.where(first, came, jnp.exp(log0[half]) * came + pair_s[half].astype(F32)))
    carry_state = jnp.concatenate(halves, axis=1)
    for b in range(NB):
        entry[b] = carry_state.astype(BF16)
        if b < NB - 1:
            carry_state = jnp.exp(totx[b, 0:1, :]) * carry_state + sblk[b]

    adj_copy.wait_recv()
    mine = adj[core]
    other = pair_a[core].astype(F32)
    a0 = jnp.where(first, mine, other)
    a1 = jnp.where(first, other, mine)
    tot_a[...] = (a0 + jnp.exp(l0) * a1).astype(BF16)

    def send_adjoint(to, carry):
        send(tot_a, ad_t.at[chip], a_s.at[to], a_r.at[chip], tm=to * 2 + core).start()
        return carry

    lax.fori_loop(0, chip, send_adjoint, 0)

    def hand_on(buf, mid, s, r, b):
        for k in range(4):
            to = b * 4 + k
            off = (to - z + N_HEAD) % N_HEAD

            @pl.when((off % 2 == 0) & (off > 0))
            def _():
                near = (z + 1 - 2 * (off // 9) + N_HEAD) % N_HEAD
                send(buf.at[to], mid.at[to], s.at[to], r.at[to], head=near).start()

    def send_sums(buf, mid, into, s, m, r):
        for off in (7, 9, 5, 11, 3, 13, 1, 15):
            to = (z + off) % N_HEAD
            if off != 9:
                send(buf.at[to], mid.at[to], s.at[to], m.at[to], head=to).wait_recv()
                buf[to] = (buf[to].astype(F32) + mid[to].astype(F32)).astype(BF16)
            send(buf.at[to], into.at[z], s.at[to], r.at[z], head=to).start()

    def local_cross(i, carry):
        b = i
        rows = block_rows(b)
        g = gy[b]
        xb = x_ref[rows, :]
        both = jnp.zeros((BLOCK, BLOCK), F32)
        into = jnp.zeros((BLOCK, BLOCK), F32)
        for h in range(NH):
            gh = g * hm[h]
            both += decay[b * NH + h] * mm_nt(gh, xb)
            into += mm_tn(scores[b * NH + h], gh)
        in_acc[b] = into
        both = both.astype(BF16)
        part = mm(both, write_ref[rows, :]) + mm_nt(gg[b], entry[b])
        for k in range(4):
            rs_r[b * 4 + k] = part[64 * k : 64 * k + 64, :].astype(BF16)
        hand_on(rs_r, mid_r, rr_s, mid_r_s, b)
        wr_acc[b] = mm_tn(both, read_ref[rows, :])
        return carry

    lax.fori_loop(0, NB, local_cross, 0)

    def pooled(b, acc):
        rows = block_rows(b)
        y = (out_acc[b] + growx[b] * mm(read_ref[rows, :], entry[b])).astype(BF16)
        return acc + mm_tn(mask[rows, :], y)

    pool = pooled(0, jnp.zeros((128, BLOCK), F32))
    ppart[...] = pool[64:96, :]
    p_copy = send(ppart, pprev, one_s.at[7], one_r.at[7], tm=prv)
    p_copy.start()
    pool = lax.fori_loop(1, NB, pooled, pool)

    send_sums(rs_r, mid_r, rr, rr_s, mid_r_s, rr_r)

    p_copy.wait_recv()
    plb[me] = ((pool[0:32, :] + pprev[...]) * inv_len).astype(BF16)

    def send_pool(d, carry):
        to = (me + d) % N_TM
        send(plb.at[me], plb.at[me], pl_s.at[to], pl_r.at[me], tm=to).start()
        return carry

    def take_adjoint(i, acc):
        m = CHIPS - 1 - i
        send(tot_a, ad_t.at[m], a_s.at[m], a_r.at[m], tm=m * 2 + core).wait_recv()
        return jnp.exp(lgt[m][0:1, :]) * acc + ad_t[m].astype(F32)

    ext[core] = lax.fori_loop(0, CHIPS - 1 - chip, take_adjoint, jnp.zeros((128, 128), F32))
    ext_copy = send(ext.at[core], ext.at[core], one_s.at[8], one_r.at[8 + core], tm=pair)
    ext_copy.start()
    lax.fori_loop(1, N_TM, send_pool, 0)
    send(ext.at[core], ext.at[1 - core], one_s.at[8], one_r.at[9 - core], tm=pair).wait_recv()
    halves = []
    for half in range(2):
        came = ext[half]
        halves.append(jnp.where(first, jnp.exp(log1[half]) * came + pair_a[half].astype(F32), came))
    carry_adj = jnp.concatenate(halves, axis=1)
    for b in range(NB - 1, -1, -1):
        leave[b] = carry_adj.astype(BF16)
        if b > 0:
            carry_adj = jnp.exp(totx[b, 0:1, :]) * carry_adj + ablk[b]

    def late_write(i, carry):
        b = i
        part = wr_acc[b] + mm_nt(xf[b], leave[b])
        for k in range(4):
            rs_w[b * 4 + k] = part[64 * k : 64 * k + 64, :].astype(BF16)
        hand_on(rs_w, mid_w, rw_s, mid_w_s, b)
        return carry

    lax.fori_loop(0, NB, late_write, 0)

    def late_inputs(b, carry):
        rows = block_rows(b)
        gi_vm[rows, :] = (in_acc[b] + fadex[b] * mm(write_ref[rows, :], leave[b])).astype(BF16)
        return carry

    lax.fori_loop(0, NB, late_inputs, 0)
    gi_copy = pltpu.make_async_copy(gi_vm, gi_ref, in_s.at[8])
    gi_copy.start()
    send_sums(rs_w, mid_w, rw, rw_s, mid_w_s, rw_r)

    def await_pool(d, carry):
        frm = (me + d) % N_TM
        send(cgat.at[0], cols.at[frm], cols_s.at[frm], cols_r.at[frm], tm=frm).wait_recv()
        send(plb.at[frm], plb.at[frm], pl_s.at[frm], pl_r.at[frm], tm=frm).wait_recv()
        return carry

    lax.fori_loop(1, N_TM, await_pool, 0)
    weight_grad = mm_tn(cols[...].reshape(N_TM * CAP, 128), plb[...].reshape(N_TM * CAP, BLOCK))
    gow_ref[...] = jnp.where(first, weight_grad[0:64, :], weight_grad[64:128, :])

    def take(buf, into, s, r):
        def step(i, acc):
            frm = (z + 2 * i + 1) % N_HEAD
            send(buf.at[frm], into.at[frm], s.at[frm], r.at[frm], head=frm).wait_recv()
            return acc + into[frm].astype(F32)

        return lax.fori_loop(0, N_HEAD // 2, step, buf[z].astype(F32))

    gr_ref[...] = take(rs_r, rr, rr_s, rr_r)
    gw_ref[...] = take(rs_w, rw, rw_s, rw_r)
    gi_copy.wait()

    for d in range(1, N_HEAD):
        send(cgat.at[z], cgat.at[z], c_s.at[d], c_r.at[z], head=(z + d) % N_HEAD).wait_send()
    for copy in (meta_copy, state_copy, lg_copy, z_copy, ent_copy, adj_copy, p_copy, ext_copy):
        copy.wait_send()

    def sent_tm(d, carry):
        to = (me + d) % N_TM
        send(cgat.at[0], cols.at[me], cols_s.at[to], cols_r.at[me], tm=to).wait_send()
        send(plb.at[me], plb.at[me], pl_s.at[to], pl_r.at[me], tm=to).wait_send()
        return carry

    def sent_log(d, carry):
        to = (chip + d) % CHIPS
        send(lgt.at[chip], lgt.at[chip], lg_s.at[to], lg_r.at[chip], tm=to * 2 + core).wait_send()
        return carry

    def sent_state(to, carry):
        send(tot_s, st_t.at[chip], t_s.at[to], t_r.at[chip], tm=to * 2 + core).wait_send()
        return carry

    def sent_adjoint(to, carry):
        send(tot_a, ad_t.at[chip], a_s.at[to], a_r.at[chip], tm=to * 2 + core).wait_send()
        return carry

    def sent_head(d, carry):
        to = (z + d) % N_HEAD
        send(rs_r.at[to], rr.at[z], rr_s.at[to], rr_r.at[z], head=to).wait_send()
        send(rs_w.at[to], rw.at[z], rw_s.at[to], rw_r.at[z], head=to).wait_send()
        return carry

    lax.fori_loop(1, N_TM, sent_tm, 0)
    lax.fori_loop(1, CHIPS, sent_log, 0)
    lax.fori_loop(chip + 1, CHIPS, sent_state, 0)
    lax.fori_loop(0, chip, sent_adjoint, 0)
    lax.fori_loop(1, N_HEAD, sent_head, 0)


def write_out(*refs):
    copies = [pltpu.make_async_copy(refs[i], refs[4 + i], refs[8].at[i]) for i in range(4)]
    for copy in copies:
        copy.start()
    for copy in copies:
        copy.wait()


def body(frame_inputs, write_map, read_map, log_decay, out_weight, caption_grad, caption_start, caption_end):
    frames, width = frame_inputs.shape
    V = pltpu.VMEM
    DMA = pltpu.SemaphoreType.DMA
    state = (2, 128, 128)
    tile = (BLOCK, BLOCK)
    scratch = [
        V(frame_inputs.shape, BF16),
        V(write_map.shape, BF16),
        V(read_map.shape, BF16),
        V(log_decay.shape, F32),
        V(out_weight.shape, BF16),
        V(caption_grad.shape, F32),
        V((1, CAP), jnp.int32),
        V((1, CAP), jnp.int32),
        DMA((9,)),
        V((N_HEAD, CAP, 128), BF16),
        V((N_TM, CAP, 128), BF16),
        V((2, 8, 128), F32),
        V((2, 8, 128), F32),
        V((CAP, BLOCK), F32),
        V((CAP, BLOCK), F32),
        V((128, BLOCK), BF16),
        V((frames, 128), BF16),
        V((NH, *tile), BF16),
        V((8, frames), F32),
        V((NB, 8, BLOCK), F32),
        V((NB, *tile), F32),
        V((NB, *tile), F32),
        V((NB, 8, BLOCK), F32),
        V((NB, *tile), BF16),
        V((NB, *tile), BF16),
        V((NB, *tile), BF16),
        V((NB, 128, BLOCK), F32),
        V((NB, 128, BLOCK), F32),
        V((NB * NH, *tile), F32),
        V((NB * NH, *tile), BF16),
        V((NB, *tile), F32),
        V((NB, *tile), F32),
        V((NB, BLOCK, 128), F32),
        V((NB, 128, BLOCK), BF16),
        V((NB, 128, BLOCK), BF16),
        V(state, F32),
        V(state, BF16),
        V(state, BF16),
        V(state, BF16),
        V(state, F32),
        V(state, BF16),
        V((2, 8, 128), F32),
        V((2, 8, 128), F32),
        V((CHIPS, 8, 128), F32),
        V((CHIPS, 128, 128), BF16),
        V((CHIPS, 128, 128), BF16),
        V((128, 128), BF16),
        V((128, 128), BF16),
        V(state, F32),
        V(state, F32),
        V((CAP, BLOCK), F32),
        V((CAP, BLOCK), F32),
        V((N_TM, CAP, BLOCK), BF16),
        V((N_HEAD, 64, 128), BF16),
        V((N_HEAD, 64, 128), BF16),
        V((N_HEAD, 64, 128), BF16),
        V((N_HEAD, 64, 128), BF16),
        V((N_HEAD, 64, 128), BF16),
        V((N_HEAD, 64, 128), BF16),
        V(frame_inputs.shape, BF16),
        DMA((N_HEAD,)),
        DMA((N_HEAD,)),
        DMA((N_TM,)),
        DMA((N_TM,)),
        DMA((10,)),
        DMA((10,)),
        DMA((CHIPS,)),
        DMA((CHIPS,)),
        DMA((CHIPS,)),
        DMA((CHIPS,)),
        DMA((CHIPS,)),
        DMA((CHIPS,)),
        DMA((N_TM,)),
        DMA((N_TM,)),
        DMA((N_HEAD,)),
        DMA((N_HEAD,)),
        DMA((N_HEAD,)),
        DMA((N_HEAD,)),
        DMA((N_HEAD,)),
        DMA((N_HEAD,)),
    ]
    vmem = pl.BlockSpec(memory_space=pltpu.VMEM)
    results = pl.pallas_call(
        kernel,
        out_shape=(
            jax.ShapeDtypeStruct((frames, width), BF16),
            jax.ShapeDtypeStruct((64, 128), F32),
            jax.ShapeDtypeStruct((64, 128), F32),
            jax.ShapeDtypeStruct((64, BLOCK), F32),
        ),
        in_specs=[pl.BlockSpec(memory_space=pltpu.HBM)] * 8,
        out_specs=(pl.BlockSpec(memory_space=pltpu.HBM), vmem, vmem, vmem),
        scratch_shapes=scratch,
        compiler_params=pltpu.CompilerParams(
            collective_id=0, has_side_effects=True, vmem_limit_bytes=63 * 1024 * 1024
        ),
    )(
        frame_inputs, write_map, read_map, log_decay, out_weight, caption_grad,
        caption_start.reshape(1, CAP), caption_end.reshape(1, CAP),
    )
    return pl.pallas_call(
        write_out,
        out_shape=tuple(jax.ShapeDtypeStruct(r.shape, r.dtype) for r in results),
        in_specs=[vmem] * 4,
        out_specs=(pl.BlockSpec(memory_space=pl.ANY),) * 4,
        scratch_shapes=[DMA((4,))],
        compiler_params=pltpu.CompilerParams(vmem_limit_bytes=62 * 1024 * 1024),
    )(*results)


def solution(mesh):
    in_specs = (
        P("tm", "head"),
        P("tm", None),
        P("tm", None),
        P("head", "tm"),
        P(None, "head"),
        P("tm", "head"),
        P("tm"),
        P("tm"),
    )
    out_specs = (P("tm", "head"), P(("tm", "head"), None), P(("tm", "head"), None), P("tm", "head"))
    return jax.shard_map(body, mesh=mesh, in_specs=in_specs, out_specs=out_specs, check_vma=False)
```

```python
import jax
import jax.numpy as jnp
from jax import lax
from jax.experimental import pallas as pl
from jax.experimental.pallas import tpu as pltpu
from jax.sharding import PartitionSpec as P

BLOCK = 256
F32 = jnp.float32
BF16 = jnp.bfloat16
MESH = pl.DeviceIdType.MESH
HIGH = lax.Precision.HIGHEST
N_TM = 32
N_HEAD = 16
CHIPS = N_TM // 2
NB = 4
NH = 4
CAP = 32
FAR_FIRST = (8, 7, 9, 6, 10, 5, 11, 4, 12, 3, 13, 2, 14, 1, 15)


def mm(a, b):
    return lax.dot_general(a, b, (((1,), (0,)), ((), ())), preferred_element_type=F32)


def mm_nt(a, b):
    return lax.dot_general(a, b, (((1,), (1,)), ((), ())), preferred_element_type=F32)


def mm_tn(a, b):
    return lax.dot_general(a, b, (((0,), (0,)), ((), ())), preferred_element_type=F32)


def block_rows(b, size=BLOCK):
    return pl.ds(pl.multiple_of(b * size, size), size)


def kernel(
    x_hbm, write_hbm, read_hbm, decay_hbm, weight_hbm, cap_hbm, start_hbm, end_hbm,
    gi_ref, gw_ref, gr_ref, gow_ref,
    x_ref, write_ref, read_ref, decay_ref, weight_ref, cap_ref, start_ref, end_ref, in_s,
    cgat, cols, meta, meta_prev, zown, zprev, zst, mask, hm,
    ld8, rowrun, growx, fadex, totx, xf, gg, gy, sblk, ablk, decay, scores,
    out_acc, wr_acc, entry, leave,
    dev, dev_b, pair_s, pair_a, adj, adj_b, lg, lg_pair, lgt, st_t, ad_t, tot_s, tot_a, ent, ext,
    next_read, next_run, grow_next, spill, spill_adj,
    ppart, pprev, plb, rs_r, rs_w, mid_r, mid_w, rr, rw, gi_vm, gw_vm, gr_vm, gow_vm,
    c_s, c_r, cols_s, cols_r, one_s, one_r, lg_s, lg_r, t_s, t_r, a_s, a_r, pl_s, pl_r, rr_s, rr_r, rw_s, rw_r, mid_r_s, mid_w_s,
):
    me = lax.axis_index("tm")
    z = lax.axis_index("head")
    chip = me // 2
    core = me % 2
    pair = me + 1 - 2 * core
    nxt = (me + 1) % N_TM
    prv = (me + N_TM - 1) % N_TM

    def send(src, dst, s, r, **where):
        return pltpu.make_async_remote_copy(
            src_ref=src, dst_ref=dst, send_sem=s, recv_sem=r, device_id=where, device_id_type=MESH
        )

    fetch = [
        pltpu.make_async_copy(src, dst, in_s.at[i])
        for i, (src, dst) in enumerate(
            (
                (cap_hbm, cap_ref),
                (start_hbm, start_ref),
                (end_hbm, end_ref),
                (decay_hbm, decay_ref),
                (x_hbm, x_ref),
                (write_hbm, write_ref),
                (read_hbm, read_ref),
                (weight_hbm, weight_ref),
            )
        )
    ]
    for copy in fetch[:7]:
        copy.start()
    barrier = pltpu.get_barrier_semaphore()

    def hail_tm(d, carry):
        pl.semaphore_signal(barrier, inc=1, device_id={"tm": (me + d) % N_TM}, device_id_type=MESH)
        return carry

    def hail_head(d, carry):
        pl.semaphore_signal(barrier, inc=1, device_id={"head": (z + d) % N_HEAD}, device_id_type=MESH)
        return carry

    for d in FAR_FIRST:
        hail_head(d, 0)
    lax.fori_loop(1, N_TM, hail_tm, 0)

    lane_head = lax.broadcasted_iota(jnp.int32, (BLOCK, BLOCK), 1) // 64
    row_id = lax.broadcasted_iota(jnp.int32, (BLOCK, BLOCK), 0)
    col_id = lax.broadcasted_iota(jnp.int32, (BLOCK, BLOCK), 1)
    for h in range(NH):
        hm[h] = (lane_head == h).astype(F32).astype(BF16)
    tri = (row_id <= col_id).astype(F32).astype(BF16)
    ld8[...] = jnp.zeros_like(ld8)
    fetch[3].wait()
    ld8[0:4, :] = decay_ref[...]
    fetch[4].wait()
    fetch[5].wait()

    def local_state(b, carry):
        rows = block_rows(b)
        left = ld8[:, rows]
        run = jnp.zeros((8, BLOCK), F32)
        for _ in range(3):
            part = left.astype(BF16)
            run += mm(part, tri)
            left = left - part.astype(F32)
        rowrun[b] = run
        col = run.T
        runx = jnp.where(
            lane_head < 2,
            jnp.where(lane_head < 1, col[:, 0:1], col[:, 1:2]),
            jnp.where(lane_head < 3, col[:, 2:3], col[:, 3:4]),
        )
        total = runx[BLOCK - 1 : BLOCK, :]
        growx[b] = jnp.exp(runx)
        fade = jnp.exp(total - runx)
        fadex[b] = fade
        totx[b] = jnp.broadcast_to(total, (8, BLOCK))
        faded = (x_ref[rows, :].astype(F32) * fade).astype(BF16)
        xf[b] = faded
        sblk[b] = mm_tn(write_ref[rows, :], faded)
        return carry

    lax.fori_loop(0, NB, local_state, 0)

    state = sblk[0]
    for b in range(1, NB):
        state = jnp.exp(totx[b, 0:1, :]) * state + sblk[b]
    log_all = totx[0] + totx[1] + totx[2] + totx[3]
    for half in range(2):
        cut = slice(128 * half, 128 * half + 128)
        dev[half] = state[:, cut]
        dev_b[half] = state[:, cut].astype(BF16)
        lg[half] = log_all[:, cut]

    fetch[0].wait()
    cgat[z] = cap_ref[...].astype(BF16)

    pl.semaphore_wait(barrier, N_TM - 1 + N_HEAD - 1)
    for d in FAR_FIRST:
        send(cgat.at[z], cgat.at[z], c_s.at[d], c_r.at[z], head=(z + d) % N_HEAD).start()
    state_copy = send(dev_b, pair_s, one_s.at[1], one_r.at[1], tm=pair)
    state_copy.start()
    lg_copy = send(lg, lg_pair, one_s.at[2], one_r.at[2], tm=pair)
    lg_copy.start()
    fetch[7].start()
    fetch[6].wait()
    rows_copy = send(read_ref.at[pl.ds(0, BLOCK)], next_read, one_s.at[5], one_r.at[10], tm=prv)
    rows_copy.start()
    run_copy = send(rowrun.at[0], next_run, one_s.at[9], one_r.at[11], tm=prv)
    run_copy.start()

    fetch[1].wait()
    fetch[2].wait()
    spread = (
        lax.broadcasted_iota(jnp.int32, (CAP, 128), 1) % CAP
        == lax.broadcasted_iota(jnp.int32, (CAP, 128), 0)
    ).astype(F32)
    start_f = start_ref[...].astype(F32)
    end_f = end_ref[...].astype(F32)
    start_row = jnp.dot(jnp.broadcast_to(start_f, (8, CAP)), spread, precision=HIGH, preferred_element_type=F32)
    end_row = jnp.dot(jnp.broadcast_to(end_f, (8, CAP)), spread, precision=HIGH, preferred_element_type=F32)
    meta[0] = start_row
    meta[1] = end_row
    eye = lax.broadcasted_iota(jnp.int32, (CAP, CAP), 0) == lax.broadcasted_iota(jnp.int32, (CAP, CAP), 1)
    inv_len = jnp.sum(jnp.where(eye, 1.0 / jnp.maximum(end_f - start_f, 1.0), 0.0), axis=1, keepdims=True)

    meta_copy = send(meta, meta_prev, one_s.at[0], one_r.at[0], tm=nxt)
    meta_copy.start()

    def local_scores(b, carry):
        rows = block_rows(b)
        both = mm_nt(read_ref[rows, :], write_ref[rows, :])
        run = rowrun[b]
        col = run.T
        xb = x_ref[rows, :]
        out = jnp.zeros((BLOCK, BLOCK), F32)
        for h in range(NH):
            gap = col[:, h : h + 1] - run[h : h + 1, :]
            dec = jnp.exp(jnp.where(row_id >= col_id, gap, -jnp.inf))
            decay[b * NH + h] = dec
            sc = (both * dec).astype(BF16)
            scores[b * NH + h] = sc
            out += mm(sc, xb * hm[h])
        out_acc[b] = out
        return carry

    lax.fori_loop(0, 2, local_scores, 0)

    state_copy.wait_recv()
    lg_copy.wait_recv()
    first = core == 0
    log0 = [jnp.where(first, lg[h], lg_pair[h])[0:1, :] for h in range(2)]
    log1 = [jnp.where(first, lg_pair[h], lg[h])[0:1, :] for h in range(2)]

    mine = dev[core]
    other = pair_s[core].astype(F32)
    s0 = jnp.where(first, mine, other)
    s1 = jnp.where(first, other, mine)
    l0 = jnp.where(first, log0[0], log0[1])
    l1 = jnp.where(first, log1[0], log1[1])
    tot_s[...] = (s1 + jnp.exp(l1) * s0).astype(BF16)
    lgt[chip] = jnp.broadcast_to(l0 + l1, (8, 128))

    def send_log(d, carry):
        to = (chip + d) % CHIPS
        send(lgt.at[chip], lgt.at[chip], lg_s.at[to], lg_r.at[chip], tm=to * 2 + core).start()
        return carry

    def send_state(to, carry):
        send(tot_s, st_t.at[chip], t_s.at[to], t_r.at[chip], tm=to * 2 + core).start()
        return carry

    lax.fori_loop(1, CHIPS, send_log, 0)
    lax.fori_loop(chip + 1, CHIPS, send_state, 0)
    lax.fori_loop(2, NB, local_scores, 0)

    meta_copy.wait_recv()
    lane = lax.broadcasted_iota(jnp.int32, (BLOCK, 128), 1)
    frame = lax.broadcasted_iota(jnp.int32, (BLOCK, 128), 0)
    seg_start = jnp.where(lane[0:8] < 64, meta[0], meta_prev[0])[0:1, :]
    seg_end = jnp.where(lane[0:8] < 64, meta[1], meta_prev[1])[0:1, :]

    def cover(b, carry):
        t = (frame + (me * (NB * BLOCK) + b * BLOCK)).astype(F32)
        inside = jnp.where(t >= seg_start, jnp.where(t < seg_end, 1.0, 0.0), 0.0)
        mask[block_rows(b), :] = inside.astype(BF16)
        return carry

    lax.fori_loop(0, NB, cover, 0)

    t = (frame + (me + 1) * (NB * BLOCK)).astype(F32)
    inside = jnp.where(t >= seg_start, jnp.where(t < seg_end, 1.0, 0.0), 0.0)
    spill[...] = jnp.where(lane < 64, inside, 0.0).astype(BF16)
    rows_copy.wait_recv()
    run_copy.wait_recv()
    col = next_run[...].T
    grow_next[...] = jnp.exp(
        jnp.where(
            lane_head < 2,
            jnp.where(lane_head < 1, col[:, 0:1], col[:, 1:2]),
            jnp.where(lane_head < 3, col[:, 2:3], col[:, 3:4]),
        )
    )

    fetch[7].wait()
    proj = mm(cgat[z], weight_ref[block_rows(z, 128), :])
    for d in (1, 15, 2, 14, 3, 13, 4, 12, 5, 11, 6, 10, 7, 9, 8):
        frm = (z + d) % N_HEAD
        send(cgat.at[frm], cgat.at[frm], c_s.at[d], c_r.at[frm], head=frm).wait_recv()
        proj += mm(cgat[frm], weight_ref[block_rows(frm, 128), :])
    proj = proj * inv_len
    zown[...] = proj
    z_copy = send(zown, zprev, one_s.at[3], one_r.at[3], tm=nxt)
    z_copy.start()

    cols[me] = cgat[chip]

    def send_cols(d, carry):
        to = (me + d) % N_TM
        send(cgat.at[to // 2], cols.at[me], cols_s.at[to], cols_r.at[me], tm=to).start()
        return carry

    lax.fori_loop(1, N_TM, send_cols, 0)

    hi = proj.astype(BF16)
    zst[0:32, :] = hi
    zst[32:64, :] = (proj - hi.astype(F32)).astype(BF16)
    zst[64:128, :] = jnp.zeros((64, BLOCK), BF16)

    def local_adjoint(i, carry):
        b = NB - 1 - i
        rows = block_rows(b)
        g = mm(mask[rows, :], zst[...]).astype(BF16)
        gy[b] = g
        grown = (g.astype(F32) * growx[b]).astype(BF16)
        gg[b] = grown
        ablk[b] = mm_tn(read_ref[rows, :], grown)
        return carry

    lax.fori_loop(0, NB, local_adjoint, 0)
    g = mm(spill[...], zst[...]).astype(BF16).astype(F32)
    spilt = mm_tn(next_read[...], (g * grow_next[...]).astype(BF16))
    spill_adj[...] = spilt
    back = ablk[NB - 1]
    for b in range(NB - 2, -1, -1):
        back = jnp.exp(totx[b, 0:1, :]) * back + ablk[b]
    back += jnp.exp(totx[0, 0:1, :] + totx[1, 0:1, :] + totx[2, 0:1, :] + totx[3, 0:1, :]) * spilt
    for half in range(2):
        cut = slice(128 * half, 128 * half + 128)
        adj[half] = back[:, cut]
        adj_b[half] = back[:, cut].astype(BF16)
    adj_copy = send(adj_b, pair_a, one_s.at[6], one_r.at[6], tm=pair)
    adj_copy.start()

    def await_log(d, carry):
        frm = (chip + d) % CHIPS
        send(lgt.at[frm], lgt.at[frm], lg_s.at[frm], lg_r.at[frm], tm=frm * 2 + core).wait_recv()
        return carry

    lax.fori_loop(1, CHIPS, await_log, 0)

    def take_state(m, acc):
        send(tot_s, st_t.at[m], t_s.at[m], t_r.at[m], tm=m * 2 + core).wait_recv()
        return jnp.exp(lgt[m][0:1, :]) * acc + st_t[m].astype(F32)

    ent[core] = lax.fori_loop(0, chip, take_state, jnp.zeros((128, 128), F32))
    ent_copy = send(ent.at[core], ent.at[core], one_s.at[4], one_r.at[4 + core], tm=pair)
    ent_copy.start()

    adj_copy.wait_recv()
    mine = adj[core]
    other = pair_a[core].astype(F32)
    a0 = jnp.where(first, mine, other)
    a1 = jnp.where(first, other, mine)
    tot_a[...] = (a0 + jnp.exp(l0) * a1).astype(BF16)

    def send_adjoint(to, carry):
        send(tot_a, ad_t.at[chip], a_s.at[to], a_r.at[chip], tm=to * 2 + core).start()
        return carry

    lax.fori_loop(0, chip, send_adjoint, 0)

    send(ent.at[core], ent.at[1 - core], one_s.at[4], one_r.at[5 - core], tm=pair).wait_recv()
    halves = []
    for half in range(2):
        came = ent[half]
        halves.append(jnp.where(first, came, jnp.exp(log0[half]) * came + pair_s[half].astype(F32)))
    carry_state = jnp.concatenate(halves, axis=1)
    for b in range(NB):
        entry[b] = carry_state.astype(BF16)
        if b < NB - 1:
            carry_state = jnp.exp(totx[b, 0:1, :]) * carry_state + sblk[b]

    def pooled(b, acc):
        rows = block_rows(b)
        y = (out_acc[b] + growx[b] * mm(read_ref[rows, :], entry[b])).astype(BF16)
        return acc + mm_tn(mask[rows, :], y)

    pool = pooled(0, jnp.zeros((128, BLOCK), F32))
    ppart[...] = pool[64:96, :]
    p_copy = send(ppart, pprev, one_s.at[7], one_r.at[7], tm=prv)
    p_copy.start()

    def hand_on(buf, mid, s, r, b):
        for k in range(4):
            to = b * 4 + k
            off = (to - z + N_HEAD) % N_HEAD

            @pl.when((off % 2 == 0) & (off > 0))
            def _():
                near = (z + 1 - 2 * (off // 9) + N_HEAD) % N_HEAD
                send(buf.at[to], mid.at[to], s.at[to], r.at[to], head=near).start()

    def send_sums(buf, mid, into, s, m, r):
        for off in (7, 9, 5, 11, 3, 13, 1, 15):
            to = (z + off) % N_HEAD
            if off != 9:
                send(buf.at[to], mid.at[to], s.at[to], m.at[to], head=to).wait_recv()
                buf[to] = (buf[to].astype(F32) + mid[to].astype(F32)).astype(BF16)
            send(buf.at[to], into.at[z], s.at[to], r.at[z], head=to).start()

    def local_cross(i, carry):
        b = NB - 1 - i
        rows = block_rows(b)
        g = gy[b]
        xb = x_ref[rows, :]
        both = jnp.zeros((BLOCK, BLOCK), F32)
        for h in range(NH):
            both += decay[b * NH + h] * mm_nt(g * hm[h], xb)
        both = both.astype(BF16)
        part = mm(both, write_ref[rows, :]) + mm_nt(gg[b], entry[b])
        for k in range(4):
            rs_r[b * 4 + k] = part[64 * k : 64 * k + 64, :].astype(BF16)
        hand_on(rs_r, mid_r, rr_s, mid_r_s, b)
        wr_acc[b] = mm_tn(both, read_ref[rows, :])
        return carry

    lax.fori_loop(0, NB - 1, local_cross, 0)
    z_copy.wait_recv()
    before = zprev[...]
    hi = before.astype(BF16)
    zst[64:96, :] = hi
    zst[96:128, :] = (before - hi.astype(F32)).astype(BF16)
    lax.fori_loop(NB - 1, NB, local_adjoint, 0)
    lax.fori_loop(NB - 1, NB, local_cross, 0)

    pool = lax.fori_loop(1, NB, pooled, pool)

    send_sums(rs_r, mid_r, rr, rr_s, mid_r_s, rr_r)

    def send_pool(d, carry):
        to = (me + d) % N_TM
        send(plb.at[me], plb.at[me], pl_s.at[to], pl_r.at[me], tm=to).start()
        return carry

    def take_adjoint(i, acc):
        m = CHIPS - 1 - i
        send(tot_a, ad_t.at[m], a_s.at[m], a_r.at[m], tm=m * 2 + core).wait_recv()
        return jnp.exp(lgt[m][0:1, :]) * acc + ad_t[m].astype(F32)

    ext[core] = lax.fori_loop(0, CHIPS - 1 - chip, take_adjoint, jnp.zeros((128, 128), F32))
    ext_copy = send(ext.at[core], ext.at[core], one_s.at[8], one_r.at[8 + core], tm=pair)
    ext_copy.start()
    send(ext.at[core], ext.at[1 - core], one_s.at[8], one_r.at[9 - core], tm=pair).wait_recv()
    halves = []
    for half in range(2):
        came = ext[half]
        halves.append(jnp.where(first, jnp.exp(log1[half]) * came + pair_a[half].astype(F32), came))
    carry_adj = jnp.concatenate(halves, axis=1) + spill_adj[...]
    for b in range(NB - 1, -1, -1):
        leave[b] = carry_adj.astype(BF16)
        if b > 0:
            carry_adj = jnp.exp(totx[b, 0:1, :]) * carry_adj + ablk[b]

    def late_write(i, carry):
        b = i
        part = wr_acc[b] + mm_nt(xf[b], leave[b])
        for k in range(4):
            rs_w[b * 4 + k] = part[64 * k : 64 * k + 64, :].astype(BF16)
        hand_on(rs_w, mid_w, rw_s, mid_w_s, b)
        return carry

    lax.fori_loop(0, NB, late_write, 0)
    p_copy.wait_recv()
    plb[me] = ((pool[0:32, :] + pprev[...]) * inv_len).astype(BF16)
    lax.fori_loop(1, N_TM, send_pool, 0)

    def late_inputs(b, carry):
        rows = block_rows(b)
        g = gy[b]
        into = fadex[b] * mm(write_ref[rows, :], leave[b])
        for h in range(NH):
            into += mm_tn(scores[b * NH + h], g * hm[h])
        gi_vm[rows, :] = into.astype(BF16)
        return carry

    lax.fori_loop(0, 2, late_inputs, 0)
    send_sums(rs_w, mid_w, rw, rw_s, mid_w_s, rw_r)
    lax.fori_loop(2, NB, late_inputs, 0)
    gi_copy = pltpu.make_async_copy(gi_vm, gi_ref, in_s.at[8])
    gi_copy.start()

    def await_pool(d, carry):
        frm = (me + d) % N_TM
        send(cgat.at[0], cols.at[frm], cols_s.at[frm], cols_r.at[frm], tm=frm).wait_recv()
        send(plb.at[frm], plb.at[frm], pl_s.at[frm], pl_r.at[frm], tm=frm).wait_recv()
        return carry

    lax.fori_loop(1, N_TM, await_pool, 0)
    weight_grad = mm_tn(cols[...].reshape(N_TM * CAP, 128), plb[...].reshape(N_TM * CAP, BLOCK))
    gow_vm[...] = jnp.where(first, weight_grad[0:64, :], weight_grad[64:128, :])
    gow_copy = pltpu.make_async_copy(gow_vm, gow_ref, in_s.at[9])
    gow_copy.start()

    def take(buf, into, s, r):
        def step(i, acc):
            frm = (z + 2 * i + 1) % N_HEAD
            send(buf.at[frm], into.at[frm], s.at[frm], r.at[frm], head=frm).wait_recv()
            return acc + into[frm].astype(F32)

        return lax.fori_loop(0, N_HEAD // 2, step, buf[z].astype(F32))

    gr_vm[...] = take(rs_r, rr, rr_s, rr_r)
    gr_copy = pltpu.make_async_copy(gr_vm, gr_ref, in_s.at[10])
    gr_copy.start()
    gw_vm[...] = take(rs_w, rw, rw_s, rw_r)
    gw_copy = pltpu.make_async_copy(gw_vm, gw_ref, in_s.at[11])
    gw_copy.start()

    for d in range(1, N_HEAD):
        send(cgat.at[z], cgat.at[z], c_s.at[d], c_r.at[z], head=(z + d) % N_HEAD).wait_send()
    for copy in (meta_copy, rows_copy, run_copy, state_copy, lg_copy, z_copy, ent_copy, adj_copy, p_copy, ext_copy):
        copy.wait_send()

    def sent_tm(d, carry):
        to = (me + d) % N_TM
        send(cgat.at[0], cols.at[me], cols_s.at[to], cols_r.at[me], tm=to).wait_send()
        send(plb.at[me], plb.at[me], pl_s.at[to], pl_r.at[me], tm=to).wait_send()
        return carry

    def sent_log(d, carry):
        to = (chip + d) % CHIPS
        send(lgt.at[chip], lgt.at[chip], lg_s.at[to], lg_r.at[chip], tm=to * 2 + core).wait_send()
        return carry

    def sent_state(to, carry):
        send(tot_s, st_t.at[chip], t_s.at[to], t_r.at[chip], tm=to * 2 + core).wait_send()
        return carry

    def sent_adjoint(to, carry):
        send(tot_a, ad_t.at[chip], a_s.at[to], a_r.at[chip], tm=to * 2 + core).wait_send()
        return carry

    def sent_head(d, carry):
        to = (z + d) % N_HEAD
        send(rs_r.at[to], rr.at[z], rr_s.at[to], rr_r.at[z], head=to).wait_send()
        send(rs_w.at[to], rw.at[z], rw_s.at[to], rw_r.at[z], head=to).wait_send()
        return carry

    lax.fori_loop(1, N_TM, sent_tm, 0)
    lax.fori_loop(1, CHIPS, sent_log, 0)
    lax.fori_loop(chip + 1, CHIPS, sent_state, 0)
    lax.fori_loop(0, chip, sent_adjoint, 0)
    lax.fori_loop(1, N_HEAD, sent_head, 0)
    for copy in (gi_copy, gow_copy, gr_copy, gw_copy):
        copy.wait()


def write_out(*refs):
    copies = [pltpu.make_async_copy(refs[i], refs[4 + i], refs[8].at[i]) for i in range(4)]
    for copy in copies:
        copy.start()
    for copy in copies:
        copy.wait()


def body(frame_inputs, write_map, read_map, log_decay, out_weight, caption_grad, caption_start, caption_end):
    frames, width = frame_inputs.shape
    V = pltpu.VMEM
    DMA = pltpu.SemaphoreType.DMA
    state = (2, 128, 128)
    tile = (BLOCK, BLOCK)
    scratch = [
        V(frame_inputs.shape, BF16),
        V(write_map.shape, BF16),
        V(read_map.shape, BF16),
        V(log_decay.shape, F32),
        V(out_weight.shape, BF16),
        V(caption_grad.shape, F32),
        V((1, CAP), jnp.int32),
        V((1, CAP), jnp.int32),
        DMA((12,)),
        V((N_HEAD, CAP, 128), BF16),
        V((N_TM, CAP, 128), BF16),
        V((2, 8, 128), F32),
        V((2, 8, 128), F32),
        V((CAP, BLOCK), F32),
        V((CAP, BLOCK), F32),
        V((128, BLOCK), BF16),
        V((frames, 128), BF16),
        V((NH, *tile), BF16),
        V((8, frames), F32),
        V((NB, 8, BLOCK), F32),
        V((NB, *tile), F32),
        V((NB, *tile), F32),
        V((NB, 8, BLOCK), F32),
        V((NB, *tile), BF16),
        V((NB, *tile), BF16),
        V((NB, *tile), BF16),
        V((NB, 128, BLOCK), F32),
        V((NB, 128, BLOCK), F32),
        V((NB * NH, *tile), F32),
        V((NB * NH, *tile), BF16),
        V((NB, *tile), F32),
        V((NB, BLOCK, 128), F32),
        V((NB, 128, BLOCK), BF16),
        V((NB, 128, BLOCK), BF16),
        V(state, F32),
        V(state, BF16),
        V(state, BF16),
        V(state, BF16),
        V(state, F32),
        V(state, BF16),
        V((2, 8, 128), F32),
        V((2, 8, 128), F32),
        V((CHIPS, 8, 128), F32),
        V((CHIPS, 128, 128), BF16),
        V((CHIPS, 128, 128), BF16),
        V((128, 128), BF16),
        V((128, 128), BF16),
        V(state, F32),
        V(state, F32),
        V((BLOCK, 128), BF16),
        V((8, BLOCK), F32),
        V(tile, F32),
        V((BLOCK, 128), BF16),
        V((128, BLOCK), F32),
        V((CAP, BLOCK), F32),
        V((CAP, BLOCK), F32),
        V((N_TM, CAP, BLOCK), BF16),
        V((N_HEAD, 64, 128), BF16),
        V((N_HEAD, 64, 128), BF16),
        V((N_HEAD, 64, 128), BF16),
        V((N_HEAD, 64, 128), BF16),
        V((N_HEAD, 64, 128), BF16),
        V((N_HEAD, 64, 128), BF16),
        V(frame_inputs.shape, BF16),
        V((64, 128), F32),
        V((64, 128), F32),
        V((64, BLOCK), F32),
        DMA((N_HEAD,)),
        DMA((N_HEAD,)),
        DMA((N_TM,)),
        DMA((N_TM,)),
        DMA((12,)),
        DMA((12,)),
        DMA((CHIPS,)),
        DMA((CHIPS,)),
        DMA((CHIPS,)),
        DMA((CHIPS,)),
        DMA((CHIPS,)),
        DMA((CHIPS,)),
        DMA((N_TM,)),
        DMA((N_TM,)),
        DMA((N_HEAD,)),
        DMA((N_HEAD,)),
        DMA((N_HEAD,)),
        DMA((N_HEAD,)),
        DMA((N_HEAD,)),
        DMA((N_HEAD,)),
    ]
    vmem = pl.BlockSpec(memory_space=pltpu.VMEM)
    results = pl.pallas_call(
        kernel,
        out_shape=(
            jax.ShapeDtypeStruct((frames, width), BF16),
            jax.ShapeDtypeStruct((64, 128), F32),
            jax.ShapeDtypeStruct((64, 128), F32),
            jax.ShapeDtypeStruct((64, BLOCK), F32),
        ),
        in_specs=[pl.BlockSpec(memory_space=pltpu.HBM)] * 8,
        out_specs=(pl.BlockSpec(memory_space=pltpu.HBM),) * 4,
        scratch_shapes=scratch,
        compiler_params=pltpu.CompilerParams(
            collective_id=0, has_side_effects=True, vmem_limit_bytes=63 * 1024 * 1024
        ),
    )(
        frame_inputs, write_map, read_map, log_decay, out_weight, caption_grad,
        caption_start.reshape(1, CAP), caption_end.reshape(1, CAP),
    )
    return pl.pallas_call(
        write_out,
        out_shape=tuple(jax.ShapeDtypeStruct(r.shape, r.dtype) for r in results),
        in_specs=[vmem] * 4,
        out_specs=(pl.BlockSpec(memory_space=pl.ANY),) * 4,
        scratch_shapes=[DMA((4,))],
        compiler_params=pltpu.CompilerParams(vmem_limit_bytes=62 * 1024 * 1024),
    )(*results)


def solution(mesh):
    in_specs = (
        P("tm", "head"),
        P("tm", None),
        P("tm", None),
        P("head", "tm"),
        P(None, "head"),
        P("tm", "head"),
        P("tm"),
        P("tm"),
    )
    out_specs = (P("tm", "head"), P(("tm", "head"), None), P(("tm", "head"), None), P("tm", "head"))
    return jax.shard_map(body, mesh=mesh, in_specs=in_specs, out_specs=out_specs, check_vma=False)
```

```python
import jax
import jax.numpy as jnp
from jax import lax
from jax.experimental import pallas as pl
from jax.experimental.pallas import tpu as pltpu
from jax.sharding import PartitionSpec as P

BLOCK = 256
F32 = jnp.float32
BF16 = jnp.bfloat16
MESH = pl.DeviceIdType.MESH
HIGH = lax.Precision.HIGHEST
N_TM = 32
N_HEAD = 16
CHIPS = N_TM // 2
NB = 4
NH = 4
CAP = 32
FAR_FIRST = (8, 7, 9, 6, 10, 5, 11, 4, 12, 3, 13, 2, 14, 1, 15)


def mm(a, b):
    return lax.dot_general(a, b, (((1,), (0,)), ((), ())), preferred_element_type=F32)


def mm_nt(a, b):
    return lax.dot_general(a, b, (((1,), (1,)), ((), ())), preferred_element_type=F32)


def mm_tn(a, b):
    return lax.dot_general(a, b, (((0,), (0,)), ((), ())), preferred_element_type=F32)


def block_rows(b, size=BLOCK):
    return pl.ds(pl.multiple_of(b * size, size), size)


def kernel(
    x_hbm, write_hbm, read_hbm, decay_hbm, weight_hbm, cap_hbm, start_hbm, end_hbm,
    gi_ref, gw_ref, gr_ref, gow_ref,
    x_ref, write_ref, read_ref, decay_ref, weight_ref, cap_ref, start_ref, end_ref, in_s,
    cgat, cols, meta, meta_prev, zown, zprev, zst, mask, hm,
    ld8, rowrun, growx, fadex, totx, xf, gg, gy, sblk, ablk, decay, scores,
    out_acc, wr_acc, entry, leave,
    dev, dev_b, pair_s, pair_a, adj, adj_b, lg, lg_pair, lgt, st_t, ad_t, tot_s, tot_a, ent, ext,
    next_read, next_run, pull, pull_next, pull_all, spill, spill_adj,
    ppart, pprev, plb, rs_r, rs_w, mid_r, mid_w, rr, rw, gi_vm, gw_vm, gr_vm, gow_vm,
    c_s, c_r, cols_s, cols_r, one_s, one_r, lg_s, lg_r, t_s, t_r, a_s, a_r, pl_s, pl_r, rr_s, rr_r, rw_s, rw_r, mid_r_s, mid_w_s,
):
    me = lax.axis_index("tm")
    z = lax.axis_index("head")
    chip = me // 2
    core = me % 2
    pair = me + 1 - 2 * core
    nxt = (me + 1) % N_TM
    prv = (me + N_TM - 1) % N_TM

    def send(src, dst, s, r, **where):
        return pltpu.make_async_remote_copy(
            src_ref=src, dst_ref=dst, send_sem=s, recv_sem=r, device_id=where, device_id_type=MESH
        )

    fetch = [
        pltpu.make_async_copy(src, dst, in_s.at[i])
        for i, (src, dst) in enumerate(
            (
                (cap_hbm, cap_ref),
                (start_hbm, start_ref),
                (end_hbm, end_ref),
                (decay_hbm, decay_ref),
                (x_hbm, x_ref),
                (write_hbm, write_ref),
                (read_hbm, read_ref),
                (weight_hbm, weight_ref),
            )
        )
    ]
    for copy in fetch[:7]:
        copy.start()
    barrier = pltpu.get_barrier_semaphore()

    def hail_tm(d, carry):
        pl.semaphore_signal(barrier, inc=1, device_id={"tm": (me + d) % N_TM}, device_id_type=MESH)
        return carry

    def hail_head(d, carry):
        pl.semaphore_signal(barrier, inc=1, device_id={"head": (z + d) % N_HEAD}, device_id_type=MESH)
        return carry

    for d in FAR_FIRST:
        hail_head(d, 0)
    lax.fori_loop(1, N_TM, hail_tm, 0)

    lane_head = lax.broadcasted_iota(jnp.int32, (BLOCK, BLOCK), 1) // 64
    row_id = lax.broadcasted_iota(jnp.int32, (BLOCK, BLOCK), 0)
    col_id = lax.broadcasted_iota(jnp.int32, (BLOCK, BLOCK), 1)
    for h in range(NH):
        hm[h] = (lane_head == h).astype(F32).astype(BF16)
    tri = (row_id <= col_id).astype(F32).astype(BF16)
    ld8[...] = jnp.zeros_like(ld8)
    fetch[3].wait()
    ld8[0:4, :] = decay_ref[...]
    fetch[4].wait()
    fetch[5].wait()

    def local_state(b, carry):
        rows = block_rows(b)
        left = ld8[:, rows]
        run = jnp.zeros((8, BLOCK), F32)
        for _ in range(3):
            part = left.astype(BF16)
            run += mm(part, tri)
            left = left - part.astype(F32)
        rowrun[b] = run
        col = run.T
        runx = jnp.where(
            lane_head < 2,
            jnp.where(lane_head < 1, col[:, 0:1], col[:, 1:2]),
            jnp.where(lane_head < 3, col[:, 2:3], col[:, 3:4]),
        )
        total = runx[BLOCK - 1 : BLOCK, :]
        growx[b] = jnp.exp(runx)
        fade = jnp.exp(total - runx)
        fadex[b] = fade
        totx[b] = jnp.broadcast_to(total, (8, BLOCK))
        faded = (x_ref[rows, :].astype(F32) * fade).astype(BF16)
        xf[b] = faded
        sblk[b] = mm_tn(write_ref[rows, :], faded)
        return carry

    lax.fori_loop(0, NB, local_state, 0)

    state = sblk[0]
    for b in range(1, NB):
        state = jnp.exp(totx[b, 0:1, :]) * state + sblk[b]
    log_all = totx[0] + totx[1] + totx[2] + totx[3]
    for half in range(2):
        cut = slice(128 * half, 128 * half + 128)
        dev[half] = state[:, cut]
        dev_b[half] = state[:, cut].astype(BF16)
        lg[half] = log_all[:, cut]

    fetch[0].wait()
    cgat[z] = cap_ref[...].astype(BF16)

    pl.semaphore_wait(barrier, N_TM - 1 + N_HEAD - 1)
    for d in FAR_FIRST:
        send(cgat.at[z], cgat.at[z], c_s.at[d], c_r.at[z], head=(z + d) % N_HEAD).start()
    state_copy = send(dev_b, pair_s, one_s.at[1], one_r.at[1], tm=pair)
    state_copy.start()
    lg_copy = send(lg, lg_pair, one_s.at[2], one_r.at[2], tm=pair)
    lg_copy.start()
    fetch[7].start()
    fetch[6].wait()
    rows_copy = send(read_ref.at[pl.ds(0, BLOCK)], next_read, one_s.at[5], one_r.at[10], tm=prv)
    rows_copy.start()
    run_copy = send(rowrun.at[0], next_run, one_s.at[9], one_r.at[11], tm=prv)
    run_copy.start()

    fetch[1].wait()
    fetch[2].wait()
    spread = (
        lax.broadcasted_iota(jnp.int32, (CAP, 128), 1) % CAP
        == lax.broadcasted_iota(jnp.int32, (CAP, 128), 0)
    ).astype(F32)
    start_f = start_ref[...].astype(F32)
    end_f = end_ref[...].astype(F32)
    start_row = jnp.dot(jnp.broadcast_to(start_f, (8, CAP)), spread, precision=HIGH, preferred_element_type=F32)
    end_row = jnp.dot(jnp.broadcast_to(end_f, (8, CAP)), spread, precision=HIGH, preferred_element_type=F32)
    meta[0] = start_row
    meta[1] = end_row
    eye = lax.broadcasted_iota(jnp.int32, (CAP, CAP), 0) == lax.broadcasted_iota(jnp.int32, (CAP, CAP), 1)
    inv_len = jnp.sum(jnp.where(eye, 1.0 / jnp.maximum(end_f - start_f, 1.0), 0.0), axis=1, keepdims=True)

    meta_copy = send(meta, meta_prev, one_s.at[0], one_r.at[0], tm=nxt)
    meta_copy.start()

    def local_scores(b, carry):
        rows = block_rows(b)
        both = mm_nt(read_ref[rows, :], write_ref[rows, :])
        run = rowrun[b]
        col = run.T
        xb = x_ref[rows, :]
        out = jnp.zeros((BLOCK, BLOCK), F32)
        for h in range(NH):
            gap = col[:, h : h + 1] - run[h : h + 1, :]
            dec = jnp.exp(jnp.where(row_id >= col_id, gap, -jnp.inf))
            decay[b * NH + h] = dec
            sc = (both * dec).astype(BF16)
            scores[b * NH + h] = sc
            out += mm(sc, xb * hm[h])
        out_acc[b] = out
        return carry

    lax.fori_loop(0, 2, local_scores, 0)

    state_copy.wait_recv()
    lg_copy.wait_recv()
    first = core == 0
    log0 = [jnp.where(first, lg[h], lg_pair[h])[0:1, :] for h in range(2)]
    log1 = [jnp.where(first, lg_pair[h], lg[h])[0:1, :] for h in range(2)]

    mine = dev[core]
    other = pair_s[core].astype(F32)
    s0 = jnp.where(first, mine, other)
    s1 = jnp.where(first, other, mine)
    l0 = jnp.where(first, log0[0], log0[1])
    l1 = jnp.where(first, log1[0], log1[1])
    tot_s[...] = (s1 + jnp.exp(l1) * s0).astype(BF16)
    lgt[chip] = jnp.broadcast_to(l0 + l1, (8, 128))

    def send_log(d, carry):
        to = (chip + d) % CHIPS
        send(lgt.at[chip], lgt.at[chip], lg_s.at[to], lg_r.at[chip], tm=to * 2 + core).start()
        return carry

    def send_state(to, carry):
        send(tot_s, st_t.at[chip], t_s.at[to], t_r.at[chip], tm=to * 2 + core).start()
        return carry

    lax.fori_loop(1, CHIPS, send_log, 0)
    lax.fori_loop(chip + 1, CHIPS, send_state, 0)
    lax.fori_loop(2, NB, local_scores, 0)

    meta_copy.wait_recv()
    lane = lax.broadcasted_iota(jnp.int32, (BLOCK, 128), 1)
    frame = lax.broadcasted_iota(jnp.int32, (BLOCK, 128), 0)
    seg_start = jnp.where(lane[0:8] < 64, meta[0], meta_prev[0])[0:1, :]
    seg_end = jnp.where(lane[0:8] < 64, meta[1], meta_prev[1])[0:1, :]

    def cover(b, carry):
        t = (frame + (me * (NB * BLOCK) + b * BLOCK)).astype(F32)
        inside = jnp.where(t >= seg_start, jnp.where(t < seg_end, 1.0, 0.0), 0.0)
        mask[block_rows(b), :] = inside.astype(BF16)
        return carry

    lax.fori_loop(0, NB, cover, 0)

    t = (frame + (me + 1) * (NB * BLOCK)).astype(F32)
    inside = jnp.where(t >= seg_start, jnp.where(t < seg_end, 1.0, 0.0), 0.0)
    spill[...] = jnp.where(lane < 64, inside, 0.0).astype(BF16)
    rows_copy.wait_recv()
    run_copy.wait_recv()
    col = next_run[...].T
    growth_next = jnp.exp(
        jnp.where(
            lane_head < 2,
            jnp.where(lane_head < 1, col[:, 0:1], col[:, 1:2]),
            jnp.where(lane_head < 3, col[:, 2:3], col[:, 3:4]),
        )
    )

    for h in range(NH):
        pull[h] = jnp.zeros((128, 128), F32)

    def local_pull(i, carry):
        b = NB - 1 - i
        rows = block_rows(b)
        grown = growx[b]
        total = totx[b, 0:1, :]
        reads = read_ref[rows, :].astype(F32)
        for h in range(NH):
            one = slice(64 * h, 64 * h + 1)
            scaled = (reads * grown[:, one]).astype(BF16)
            pull[h] = jnp.exp(total[:, one]) * pull[h] + mm_tn(scaled, mask[rows, :])
        return carry

    lax.fori_loop(0, NB, local_pull, 0)
    dev_log = totx[0, 0:1, :] + totx[1, 0:1, :] + totx[2, 0:1, :] + totx[3, 0:1, :]
    reads = next_read[...].astype(F32)
    for h in range(NH):
        one = slice(64 * h, 64 * h + 1)
        scaled = (reads * growth_next[:, one]).astype(BF16)
        part = mm_tn(scaled, spill[...])
        pull_next[h] = part.astype(BF16)
        pull_all[h] = (pull[h] + jnp.exp(dev_log[:, one]) * part).astype(BF16)

    fetch[7].wait()
    proj = mm(cgat[z], weight_ref[block_rows(z, 128), :])
    for d in (1, 15, 2, 14, 3, 13, 4, 12, 5, 11, 6, 10, 7, 9, 8):
        frm = (z + d) % N_HEAD
        send(cgat.at[frm], cgat.at[frm], c_s.at[d], c_r.at[frm], head=frm).wait_recv()
        proj += mm(cgat[frm], weight_ref[block_rows(frm, 128), :])
    proj = proj * inv_len
    zown[...] = proj
    z_copy = send(zown, zprev, one_s.at[3], one_r.at[3], tm=nxt)
    z_copy.start()

    hi = proj.astype(BF16)
    zst[0:32, :] = hi
    zst[32:64, :] = (proj - hi.astype(F32)).astype(BF16)
    zst[64:128, :] = jnp.zeros((64, BLOCK), BF16)

    rows_z = [zst[...] * hm[h, 0:128, :] for h in range(NH)]
    back = mm(pull_all[0], rows_z[0])
    for h in range(1, NH):
        back += mm(pull_all[h], rows_z[h])
    for half in range(2):
        cut = slice(128 * half, 128 * half + 128)
        adj[half] = back[:, cut]
        adj_b[half] = back[:, cut].astype(BF16)
    adj_copy = send(adj_b, pair_a, one_s.at[6], one_r.at[6], tm=pair)
    adj_copy.start()
    spilt = mm(pull_next[0], rows_z[0])
    for h in range(1, NH):
        spilt += mm(pull_next[h], rows_z[h])
    spill_adj[...] = spilt

    cols[me] = cgat[chip]

    def send_cols(d, carry):
        to = (me + d) % N_TM
        send(cgat.at[to // 2], cols.at[me], cols_s.at[to], cols_r.at[me], tm=to).start()
        return carry

    lax.fori_loop(1, N_TM, send_cols, 0)

    def await_log(d, carry):
        frm = (chip + d) % CHIPS
        send(lgt.at[frm], lgt.at[frm], lg_s.at[frm], lg_r.at[frm], tm=frm * 2 + core).wait_recv()
        return carry

    lax.fori_loop(1, CHIPS, await_log, 0)

    def take_state(m, acc):
        send(tot_s, st_t.at[m], t_s.at[m], t_r.at[m], tm=m * 2 + core).wait_recv()
        return jnp.exp(lgt[m][0:1, :]) * acc + st_t[m].astype(F32)

    ent[core] = lax.fori_loop(0, chip, take_state, jnp.zeros((128, 128), F32))
    ent_copy = send(ent.at[core], ent.at[core], one_s.at[4], one_r.at[4 + core], tm=pair)
    ent_copy.start()

    adj_copy.wait_recv()
    mine = adj[core]
    other = pair_a[core].astype(F32)
    a0 = jnp.where(first, mine, other)
    a1 = jnp.where(first, other, mine)
    tot_a[...] = (a0 + jnp.exp(l0) * a1).astype(BF16)

    def send_adjoint(to, carry):
        send(tot_a, ad_t.at[chip], a_s.at[to], a_r.at[chip], tm=to * 2 + core).start()
        return carry

    lax.fori_loop(0, chip, send_adjoint, 0)

    send(ent.at[core], ent.at[1 - core], one_s.at[4], one_r.at[5 - core], tm=pair).wait_recv()
    halves = []
    for half in range(2):
        came = ent[half]
        halves.append(jnp.where(first, came, jnp.exp(log0[half]) * came + pair_s[half].astype(F32)))
    carry_state = jnp.concatenate(halves, axis=1)
    for b in range(NB):
        entry[b] = carry_state.astype(BF16)
        if b < NB - 1:
            carry_state = jnp.exp(totx[b, 0:1, :]) * carry_state + sblk[b]

    def hand_on(buf, mid, s, r, b):
        for k in range(4):
            to = b * 4 + k
            off = (to - z + N_HEAD) % N_HEAD

            @pl.when((off % 2 == 0) & (off > 0))
            def _():
                near = (z + 1 - 2 * (off // 9) + N_HEAD) % N_HEAD
                send(buf.at[to], mid.at[to], s.at[to], r.at[to], head=near).start()

    def send_sums(buf, mid, into, s, m, r):
        for off in (7, 9, 5, 11, 3, 13, 1, 15):
            to = (z + off) % N_HEAD
            if off != 9:
                send(buf.at[to], mid.at[to], s.at[to], m.at[to], head=to).wait_recv()
                buf[to] = (buf[to].astype(F32) + mid[to].astype(F32)).astype(BF16)
            send(buf.at[to], into.at[z], s.at[to], r.at[z], head=to).start()

    def local_adjoint(i, carry):
        b = NB - 1 - i
        rows = block_rows(b)
        g = mm(mask[rows, :], zst[...]).astype(BF16)
        gy[b] = g
        grown = (g.astype(F32) * growx[b]).astype(BF16)
        gg[b] = grown
        return carry

    def block_adjoint(i, carry):
        b = NB - 1 - i
        ablk[b] = mm_tn(read_ref[block_rows(b), :], gg[b])
        return carry

    def local_cross(i, carry):
        b = NB - 1 - i
        rows = block_rows(b)
        g = gy[b]
        xb = x_ref[rows, :]
        both = jnp.zeros((BLOCK, BLOCK), F32)
        for h in range(NH):
            both += decay[b * NH + h] * mm_nt(g * hm[h], xb)
        both = both.astype(BF16)
        part = mm(both, write_ref[rows, :]) + mm_nt(gg[b], entry[b])
        for k in range(4):
            rs_r[b * 4 + k] = part[64 * k : 64 * k + 64, :].astype(BF16)
        hand_on(rs_r, mid_r, rr_s, mid_r_s, b)
        wr_acc[b] = mm_tn(both, read_ref[rows, :])
        return carry

    def cotangent_and_cross(i, carry):
        return local_cross(i, local_adjoint(i, carry))

    lax.fori_loop(0, NB - 1, cotangent_and_cross, 0)
    z_copy.wait_recv()
    before = zprev[...]
    hi = before.astype(BF16)
    zst[64:96, :] = hi
    zst[96:128, :] = (before - hi.astype(F32)).astype(BF16)
    lax.fori_loop(NB - 1, NB, cotangent_and_cross, 0)

    def pooled(b, acc):
        rows = block_rows(b)
        y = (out_acc[b] + growx[b] * mm(read_ref[rows, :], entry[b])).astype(BF16)
        return acc + mm_tn(mask[rows, :], y)

    pool = pooled(0, jnp.zeros((128, BLOCK), F32))
    ppart[...] = pool[64:96, :]
    p_copy = send(ppart, pprev, one_s.at[7], one_r.at[7], tm=prv)
    p_copy.start()

    pool = lax.fori_loop(1, NB, pooled, pool)
    lax.fori_loop(0, NB - 1, block_adjoint, 0)

    send_sums(rs_r, mid_r, rr, rr_s, mid_r_s, rr_r)

    def send_pool(d, carry):
        to = (me + d) % N_TM
        send(plb.at[me], plb.at[me], pl_s.at[to], pl_r.at[me], tm=to).start()
        return carry

    def take_adjoint(i, acc):
        m = CHIPS - 1 - i
        send(tot_a, ad_t.at[m], a_s.at[m], a_r.at[m], tm=m * 2 + core).wait_recv()
        return jnp.exp(lgt[m][0:1, :]) * acc + ad_t[m].astype(F32)

    ext[core] = lax.fori_loop(0, CHIPS - 1 - chip, take_adjoint, jnp.zeros((128, 128), F32))
    ext_copy = send(ext.at[core], ext.at[core], one_s.at[8], one_r.at[8 + core], tm=pair)
    ext_copy.start()
    send(ext.at[core], ext.at[1 - core], one_s.at[8], one_r.at[9 - core], tm=pair).wait_recv()
    halves = []
    for half in range(2):
        came = ext[half]
        halves.append(jnp.where(first, jnp.exp(log1[half]) * came + pair_a[half].astype(F32), came))
    carry_adj = jnp.concatenate(halves, axis=1) + spill_adj[...]
    for b in range(NB - 1, -1, -1):
        leave[b] = carry_adj.astype(BF16)
        if b > 0:
            carry_adj = jnp.exp(totx[b, 0:1, :]) * carry_adj + ablk[b]

    def late_write(i, carry):
        b = i
        part = wr_acc[b] + mm_nt(xf[b], leave[b])
        for k in range(4):
            rs_w[b * 4 + k] = part[64 * k : 64 * k + 64, :].astype(BF16)
        hand_on(rs_w, mid_w, rw_s, mid_w_s, b)
        return carry

    lax.fori_loop(0, NB, late_write, 0)
    p_copy.wait_recv()
    plb[me] = ((pool[0:32, :] + pprev[...]) * inv_len).astype(BF16)
    lax.fori_loop(1, N_TM, send_pool, 0)

    def late_inputs(b, carry):
        rows = block_rows(b)
        g = gy[b]
        into = fadex[b] * mm(write_ref[rows, :], leave[b])
        for h in range(NH):
            into += mm_tn(scores[b * NH + h], g * hm[h])
        gi_vm[rows, :] = into.astype(BF16)
        return carry

    lax.fori_loop(0, 2, late_inputs, 0)
    send_sums(rs_w, mid_w, rw, rw_s, mid_w_s, rw_r)
    lax.fori_loop(2, NB, late_inputs, 0)
    gi_copy = pltpu.make_async_copy(gi_vm, gi_ref, in_s.at[8])
    gi_copy.start()

    def await_pool(d, carry):
        frm = (me + d) % N_TM
        send(cgat.at[0], cols.at[frm], cols_s.at[frm], cols_r.at[frm], tm=frm).wait_recv()
        send(plb.at[frm], plb.at[frm], pl_s.at[frm], pl_r.at[frm], tm=frm).wait_recv()
        return carry

    lax.fori_loop(1, N_TM, await_pool, 0)
    weight_grad = mm_tn(cols[...].reshape(N_TM * CAP, 128), plb[...].reshape(N_TM * CAP, BLOCK))
    gow_vm[...] = jnp.where(first, weight_grad[0:64, :], weight_grad[64:128, :])
    gow_copy = pltpu.make_async_copy(gow_vm, gow_ref, in_s.at[9])
    gow_copy.start()

    def take(buf, into, s, r):
        def step(i, acc):
            frm = (z + 2 * i + 1) % N_HEAD
            send(buf.at[frm], into.at[frm], s.at[frm], r.at[frm], head=frm).wait_recv()
            return acc + into[frm].astype(F32)

        return lax.fori_loop(0, N_HEAD // 2, step, buf[z].astype(F32))

    gr_vm[...] = take(rs_r, rr, rr_s, rr_r)
    gr_copy = pltpu.make_async_copy(gr_vm, gr_ref, in_s.at[10])
    gr_copy.start()

    for d in range(1, N_HEAD):
        send(cgat.at[z], cgat.at[z], c_s.at[d], c_r.at[z], head=(z + d) % N_HEAD).wait_send()
    for copy in (meta_copy, rows_copy, run_copy, state_copy, lg_copy, z_copy, ent_copy, adj_copy, p_copy, ext_copy):
        copy.wait_send()

    def sent_tm(d, carry):
        to = (me + d) % N_TM
        send(cgat.at[0], cols.at[me], cols_s.at[to], cols_r.at[me], tm=to).wait_send()
        send(plb.at[me], plb.at[me], pl_s.at[to], pl_r.at[me], tm=to).wait_send()
        return carry

    def sent_log(d, carry):
        to = (chip + d) % CHIPS
        send(lgt.at[chip], lgt.at[chip], lg_s.at[to], lg_r.at[chip], tm=to * 2 + core).wait_send()
        return carry

    def sent_state(to, carry):
        send(tot_s, st_t.at[chip], t_s.at[to], t_r.at[chip], tm=to * 2 + core).wait_send()
        return carry

    def sent_adjoint(to, carry):
        send(tot_a, ad_t.at[chip], a_s.at[to], a_r.at[chip], tm=to * 2 + core).wait_send()
        return carry

    lax.fori_loop(1, N_TM, sent_tm, 0)
    lax.fori_loop(1, CHIPS, sent_log, 0)
    lax.fori_loop(chip + 1, CHIPS, sent_state, 0)
    lax.fori_loop(0, chip, sent_adjoint, 0)

    gw_vm[...] = take(rs_w, rw, rw_s, rw_r)
    gw_copy = pltpu.make_async_copy(gw_vm, gw_ref, in_s.at[11])
    gw_copy.start()

    def sent_head(d, carry):
        to = (z + d) % N_HEAD
        send(rs_r.at[to], rr.at[z], rr_s.at[to], rr_r.at[z], head=to).wait_send()
        send(rs_w.at[to], rw.at[z], rw_s.at[to], rw_r.at[z], head=to).wait_send()
        return carry

    lax.fori_loop(1, N_HEAD, sent_head, 0)
    for copy in (gi_copy, gow_copy, gr_copy, gw_copy):
        copy.wait()


def write_out(gi, gw, gr, gow, gi_out, gw_out, gr_out, gow_out, gi_vm, gw_vm, gr_vm, gow_vm, came, left):
    size = gi.shape[0] // 4
    moves = [(gi.at[pl.ds(i * size, size)], gi_vm.at[pl.ds(i * size, size)], gi_out.at[pl.ds(i * size, size)]) for i in range(4)]
    moves += [(gw, gw_vm, gw_out), (gr, gr_vm, gr_out), (gow, gow_vm, gow_out)]
    ins = [pltpu.make_async_copy(a, b, came.at[i]) for i, (a, b, _) in enumerate(moves)]
    outs = [pltpu.make_async_copy(b, c, left.at[i]) for i, (_, b, c) in enumerate(moves)]
    for copy in ins:
        copy.start()
    for here, there in zip(ins, outs):
        here.wait()
        there.start()
    for copy in outs:
        copy.wait()


def body(frame_inputs, write_map, read_map, log_decay, out_weight, caption_grad, caption_start, caption_end):
    frames, width = frame_inputs.shape
    V = pltpu.VMEM
    DMA = pltpu.SemaphoreType.DMA
    state = (2, 128, 128)
    tile = (BLOCK, BLOCK)
    scratch = [
        V(frame_inputs.shape, BF16),
        V(write_map.shape, BF16),
        V(read_map.shape, BF16),
        V(log_decay.shape, F32),
        V(out_weight.shape, BF16),
        V(caption_grad.shape, F32),
        V((1, CAP), jnp.int32),
        V((1, CAP), jnp.int32),
        DMA((12,)),
        V((N_HEAD, CAP, 128), BF16),
        V((N_TM, CAP, 128), BF16),
        V((2, 8, 128), F32),
        V((2, 8, 128), F32),
        V((CAP, BLOCK), F32),
        V((CAP, BLOCK), F32),
        V((128, BLOCK), BF16),
        V((frames, 128), BF16),
        V((NH, *tile), BF16),
        V((8, frames), F32),
        V((NB, 8, BLOCK), F32),
        V((NB, *tile), F32),
        V((NB, *tile), F32),
        V((NB, 8, BLOCK), F32),
        V((NB, *tile), BF16),
        V((NB, *tile), BF16),
        V((NB, *tile), BF16),
        V((NB, 128, BLOCK), F32),
        V((NB, 128, BLOCK), F32),
        V((NB * NH, *tile), F32),
        V((NB * NH, *tile), BF16),
        V((NB, *tile), F32),
        V((NB, BLOCK, 128), F32),
        V((NB, 128, BLOCK), BF16),
        V((NB, 128, BLOCK), BF16),
        V(state, F32),
        V(state, BF16),
        V(state, BF16),
        V(state, BF16),
        V(state, F32),
        V(state, BF16),
        V((2, 8, 128), F32),
        V((2, 8, 128), F32),
        V((CHIPS, 8, 128), F32),
        V((CHIPS, 128, 128), BF16),
        V((CHIPS, 128, 128), BF16),
        V((128, 128), BF16),
        V((128, 128), BF16),
        V(state, F32),
        V(state, F32),
        V((BLOCK, 128), BF16),
        V((8, BLOCK), F32),
        V((NH, 128, 128), F32),
        V((NH, 128, 128), BF16),
        V((NH, 128, 128), BF16),
        V((BLOCK, 128), BF16),
        V((128, BLOCK), F32),
        V((CAP, BLOCK), F32),
        V((CAP, BLOCK), F32),
        V((N_TM, CAP, BLOCK), BF16),
        V((N_HEAD, 64, 128), BF16),
        V((N_HEAD, 64, 128), BF16),
        V((N_HEAD, 64, 128), BF16),
        V((N_HEAD, 64, 128), BF16),
        V((N_HEAD, 64, 128), BF16),
        V((N_HEAD, 64, 128), BF16),
        V(frame_inputs.shape, BF16),
        V((64, 128), F32),
        V((64, 128), F32),
        V((64, BLOCK), F32),
        DMA((N_HEAD,)),
        DMA((N_HEAD,)),
        DMA((N_TM,)),
        DMA((N_TM,)),
        DMA((12,)),
        DMA((12,)),
        DMA((CHIPS,)),
        DMA((CHIPS,)),
        DMA((CHIPS,)),
        DMA((CHIPS,)),
        DMA((CHIPS,)),
        DMA((CHIPS,)),
        DMA((N_TM,)),
        DMA((N_TM,)),
        DMA((N_HEAD,)),
        DMA((N_HEAD,)),
        DMA((N_HEAD,)),
        DMA((N_HEAD,)),
        DMA((N_HEAD,)),
        DMA((N_HEAD,)),
    ]
    results = pl.pallas_call(
        kernel,
        out_shape=(
            jax.ShapeDtypeStruct((frames, width), BF16),
            jax.ShapeDtypeStruct((64, 128), F32),
            jax.ShapeDtypeStruct((64, 128), F32),
            jax.ShapeDtypeStruct((64, BLOCK), F32),
        ),
        in_specs=[pl.BlockSpec(memory_space=pltpu.HBM)] * 8,
        out_specs=(pl.BlockSpec(memory_space=pltpu.HBM),) * 4,
        scratch_shapes=scratch,
        compiler_params=pltpu.CompilerParams(
            collective_id=0, has_side_effects=True, vmem_limit_bytes=63 * 1024 * 1024
        ),
    )(
        frame_inputs, write_map, read_map, log_decay, out_weight, caption_grad,
        caption_start.reshape(1, CAP), caption_end.reshape(1, CAP),
    )
    return pl.pallas_call(
        write_out,
        out_shape=tuple(jax.ShapeDtypeStruct(r.shape, r.dtype) for r in results),
        in_specs=[pl.BlockSpec(memory_space=pltpu.HBM)] * 4,
        out_specs=(pl.BlockSpec(memory_space=pltpu.HBM),) * 4,
        scratch_shapes=[V(r.shape, r.dtype) for r in results] + [DMA((7,)), DMA((7,))],
        compiler_params=pltpu.CompilerParams(vmem_limit_bytes=62 * 1024 * 1024),
    )(*results)


def solution(mesh):
    in_specs = (
        P("tm", "head"),
        P("tm", None),
        P("tm", None),
        P("head", "tm"),
        P(None, "head"),
        P("tm", "head"),
        P("tm"),
        P("tm"),
    )
    out_specs = (P("tm", "head"), P(("tm", "head"), None), P(("tm", "head"), None), P("tm", "head"))
    return jax.shard_map(body, mesh=mesh, in_specs=in_specs, out_specs=out_specs, check_vma=False)
```

```python
import jax
import jax.numpy as jnp
from jax import lax
from jax.experimental import pallas as pl
from jax.experimental.pallas import tpu as pltpu
from jax.sharding import PartitionSpec as P

BLOCK = 256
F32 = jnp.float32
BF16 = jnp.bfloat16
MESH = pl.DeviceIdType.MESH
HIGH = lax.Precision.HIGHEST
N_TM = 32
N_HEAD = 16
CHIPS = N_TM // 2
NB = 4
NH = 4
CAP = 32
FAR_FIRST = (8, 7, 9, 6, 10, 5, 11, 4, 12, 3, 13, 2, 14, 1, 15)


def mm(a, b):
    return lax.dot_general(a, b, (((1,), (0,)), ((), ())), preferred_element_type=F32)


def mm_nt(a, b):
    return lax.dot_general(a, b, (((1,), (1,)), ((), ())), preferred_element_type=F32)


def mm_tn(a, b):
    return lax.dot_general(a, b, (((0,), (0,)), ((), ())), preferred_element_type=F32)


def block_rows(b, size=BLOCK):
    return pl.ds(pl.multiple_of(b * size, size), size)


def kernel(
    x_hbm, write_hbm, read_hbm, decay_hbm, weight_hbm, cap_hbm, start_hbm, end_hbm,
    gi_ref, gw_ref, gr_ref, gow_ref,
    x_ref, write_ref, read_ref, decay_ref, weight_ref, cap_ref, start_ref, end_ref, in_s,
    cgat, cols, meta, meta_prev, zown, zprev, zst, mask, hm,
    ld8, rowrun, growx, fadex, totx, xf, gg, gy, sblk, ablk, decay, scores,
    out_acc, wr_acc, entry, leave,
    dev, dev_b, pair_s, pair_a, adj, adj_b, lg, lg_pair, lgt, st_t, ad_t, tot_s, tot_a, ent, ext,
    next_read, next_run, pull, pull_next, pull_all, spill, spill_adj,
    ppart, pprev, plb, rs_r, rs_w, mid_r, mid_w, rr, rw, gi_vm, gw_vm, gr_vm, gow_vm,
    c_s, c_r, cols_s, cols_r, one_s, one_r, lg_s, lg_r, t_s, t_r, a_s, a_r, pl_s, pl_r, rr_s, rr_r, rw_s, rw_r, mid_r_s, mid_w_s,
):
    me = lax.axis_index("tm")
    z = lax.axis_index("head")
    chip = me // 2
    core = me % 2
    pair = me + 1 - 2 * core
    nxt = (me + 1) % N_TM
    prv = (me + N_TM - 1) % N_TM

    def send(src, dst, s, r, **where):
        return pltpu.make_async_remote_copy(
            src_ref=src, dst_ref=dst, send_sem=s, recv_sem=r, device_id=where, device_id_type=MESH
        )

    fetch = [
        pltpu.make_async_copy(src, dst, in_s.at[i])
        for i, (src, dst) in enumerate(
            (
                (cap_hbm, cap_ref),
                (start_hbm, start_ref),
                (end_hbm, end_ref),
                (decay_hbm, decay_ref),
                (x_hbm, x_ref),
                (write_hbm, write_ref),
                (read_hbm, read_ref),
                (weight_hbm, weight_ref),
            )
        )
    ]
    for copy in fetch[:7]:
        copy.start()
    barrier = pltpu.get_barrier_semaphore()

    def hail_tm(d, carry):
        pl.semaphore_signal(barrier, inc=1, device_id={"tm": (me + d) % N_TM}, device_id_type=MESH)
        return carry

    def hail_head(d, carry):
        pl.semaphore_signal(barrier, inc=1, device_id={"head": (z + d) % N_HEAD}, device_id_type=MESH)
        return carry

    for d in FAR_FIRST:
        hail_head(d, 0)
    lax.fori_loop(1, N_TM, hail_tm, 0)

    lane_head = lax.broadcasted_iota(jnp.int32, (BLOCK, BLOCK), 1) // 64
    row_id = lax.broadcasted_iota(jnp.int32, (BLOCK, BLOCK), 0)
    col_id = lax.broadcasted_iota(jnp.int32, (BLOCK, BLOCK), 1)
    for h in range(NH):
        hm[h] = (lane_head == h).astype(F32).astype(BF16)
    tri = (row_id <= col_id).astype(F32).astype(BF16)
    ld8[...] = jnp.zeros_like(ld8)
    fetch[3].wait()
    ld8[0:4, :] = decay_ref[...]
    fetch[4].wait()
    fetch[5].wait()

    def local_state(b, carry):
        rows = block_rows(b)
        left = ld8[:, rows]
        run = jnp.zeros((8, BLOCK), F32)
        for _ in range(3):
            part = left.astype(BF16)
            run += mm(part, tri)
            left = left - part.astype(F32)
        rowrun[b] = run
        col = run.T
        runx = jnp.where(
            lane_head < 2,
            jnp.where(lane_head < 1, col[:, 0:1], col[:, 1:2]),
            jnp.where(lane_head < 3, col[:, 2:3], col[:, 3:4]),
        )
        total = runx[BLOCK - 1 : BLOCK, :]
        growx[b] = jnp.exp(runx)
        fade = jnp.exp(total - runx)
        fadex[b] = fade
        totx[b] = jnp.broadcast_to(total, (8, BLOCK))
        faded = (x_ref[rows, :].astype(F32) * fade).astype(BF16)
        xf[b] = faded
        sblk[b] = mm_tn(write_ref[rows, :], faded)
        return carry

    lax.fori_loop(0, NB, local_state, 0)

    state = sblk[0]
    for b in range(1, NB):
        state = jnp.exp(totx[b, 0:1, :]) * state + sblk[b]
    log_all = totx[0] + totx[1] + totx[2] + totx[3]
    for half in range(2):
        cut = slice(128 * half, 128 * half + 128)
        dev[half] = state[:, cut]
        dev_b[half] = state[:, cut].astype(BF16)
        lg[half] = log_all[:, cut]

    fetch[0].wait()
    cgat[z] = cap_ref[...].astype(BF16)

    pl.semaphore_wait(barrier, N_TM - 1 + N_HEAD - 1)
    for d in FAR_FIRST:
        send(cgat.at[z], cgat.at[z], c_s.at[d], c_r.at[z], head=(z + d) % N_HEAD).start()
    state_copy = send(dev_b, pair_s, one_s.at[1], one_r.at[1], tm=pair)
    state_copy.start()
    lg_copy = send(lg, lg_pair, one_s.at[2], one_r.at[2], tm=pair)
    lg_copy.start()
    fetch[7].start()
    fetch[6].wait()
    rows_copy = send(read_ref.at[pl.ds(0, BLOCK)], next_read, one_s.at[5], one_r.at[10], tm=prv)
    rows_copy.start()
    run_copy = send(rowrun.at[0], next_run, one_s.at[9], one_r.at[11], tm=prv)
    run_copy.start()

    fetch[1].wait()
    fetch[2].wait()
    spread = (
        lax.broadcasted_iota(jnp.int32, (CAP, 128), 1) % CAP
        == lax.broadcasted_iota(jnp.int32, (CAP, 128), 0)
    ).astype(F32)
    start_f = start_ref[...].astype(F32)
    end_f = end_ref[...].astype(F32)
    start_row = jnp.dot(jnp.broadcast_to(start_f, (8, CAP)), spread, precision=HIGH, preferred_element_type=F32)
    end_row = jnp.dot(jnp.broadcast_to(end_f, (8, CAP)), spread, precision=HIGH, preferred_element_type=F32)
    meta[0] = start_row
    meta[1] = end_row
    eye = lax.broadcasted_iota(jnp.int32, (CAP, CAP), 0) == lax.broadcasted_iota(jnp.int32, (CAP, CAP), 1)
    inv_len = jnp.sum(jnp.where(eye, 1.0 / jnp.maximum(end_f - start_f, 1.0), 0.0), axis=1, keepdims=True)

    meta_copy = send(meta, meta_prev, one_s.at[0], one_r.at[0], tm=nxt)
    meta_copy.start()

    def local_scores(b, carry):
        rows = block_rows(b)
        both = mm_nt(read_ref[rows, :], write_ref[rows, :])
        run = rowrun[b]
        col = run.T
        xb = x_ref[rows, :]
        out = jnp.zeros((BLOCK, BLOCK), F32)
        for h in range(NH):
            gap = col[:, h : h + 1] - run[h : h + 1, :]
            dec = jnp.exp(jnp.where(row_id >= col_id, gap, -jnp.inf))
            decay[b * NH + h] = dec
            sc = (both * dec).astype(BF16)
            scores[b * NH + h] = sc
            out += mm(sc, xb * hm[h])
        out_acc[b] = out
        return carry

    lax.fori_loop(0, 2, local_scores, 0)

    state_copy.wait_recv()
    lg_copy.wait_recv()
    first = core == 0
    log0 = [jnp.where(first, lg[h], lg_pair[h])[0:1, :] for h in range(2)]
    log1 = [jnp.where(first, lg_pair[h], lg[h])[0:1, :] for h in range(2)]

    mine = dev[core]
    other = pair_s[core].astype(F32)
    s0 = jnp.where(first, mine, other)
    s1 = jnp.where(first, other, mine)
    l0 = jnp.where(first, log0[0], log0[1])
    l1 = jnp.where(first, log1[0], log1[1])
    tot_s[...] = (s1 + jnp.exp(l1) * s0).astype(BF16)
    lgt[chip] = jnp.broadcast_to(l0 + l1, (8, 128))

    def send_log(d, carry):
        to = (chip + d) % CHIPS
        send(lgt.at[chip], lgt.at[chip], lg_s.at[to], lg_r.at[chip], tm=to * 2 + core).start()
        return carry

    def send_state(to, carry):
        send(tot_s, st_t.at[chip], t_s.at[to], t_r.at[chip], tm=to * 2 + core).start()
        return carry

    lax.fori_loop(1, CHIPS, send_log, 0)
    lax.fori_loop(chip + 1, CHIPS, send_state, 0)
    lax.fori_loop(2, NB, local_scores, 0)

    meta_copy.wait_recv()
    lane = lax.broadcasted_iota(jnp.int32, (BLOCK, 128), 1)
    frame = lax.broadcasted_iota(jnp.int32, (BLOCK, 128), 0)
    seg_start = jnp.where(lane[0:8] < 64, meta[0], meta_prev[0])[0:1, :]
    seg_end = jnp.where(lane[0:8] < 64, meta[1], meta_prev[1])[0:1, :]

    def cover(b, carry):
        t = (frame + (me * (NB * BLOCK) + b * BLOCK)).astype(F32)
        inside = jnp.where(t >= seg_start, jnp.where(t < seg_end, 1.0, 0.0), 0.0)
        mask[block_rows(b), :] = inside.astype(BF16)
        return carry

    lax.fori_loop(0, NB, cover, 0)

    t = (frame + (me + 1) * (NB * BLOCK)).astype(F32)
    inside = jnp.where(t >= seg_start, jnp.where(t < seg_end, 1.0, 0.0), 0.0)
    spill[...] = jnp.where(lane < 64, inside, 0.0).astype(BF16)
    rows_copy.wait_recv()
    run_copy.wait_recv()
    col = next_run[...].T
    growth_next = jnp.exp(
        jnp.where(
            lane_head < 2,
            jnp.where(lane_head < 1, col[:, 0:1], col[:, 1:2]),
            jnp.where(lane_head < 3, col[:, 2:3], col[:, 3:4]),
        )
    )

    for h in range(NH):
        pull[h] = jnp.zeros((128, 128), F32)

    def local_pull(i, carry):
        b = NB - 1 - i
        rows = block_rows(b)
        grown = growx[b]
        total = totx[b, 0:1, :]
        reads = read_ref[rows, :].astype(F32)
        for h in range(NH):
            one = slice(64 * h, 64 * h + 1)
            scaled = (reads * grown[:, one]).astype(BF16)
            pull[h] = jnp.exp(total[:, one]) * pull[h] + mm_tn(scaled, mask[rows, :])
        return carry

    lax.fori_loop(0, NB, local_pull, 0)
    dev_log = totx[0, 0:1, :] + totx[1, 0:1, :] + totx[2, 0:1, :] + totx[3, 0:1, :]
    reads = next_read[...].astype(F32)
    for h in range(NH):
        one = slice(64 * h, 64 * h + 1)
        scaled = (reads * growth_next[:, one]).astype(BF16)
        part = mm_tn(scaled, spill[...])
        pull_next[h] = part.astype(BF16)
        pull_all[h] = (pull[h] + jnp.exp(dev_log[:, one]) * part).astype(BF16)

    fetch[7].wait()
    proj = mm(cgat[z], weight_ref[block_rows(z, 128), :])
    for d in (1, 15, 2, 14, 3, 13, 4, 12, 5, 11, 6, 10, 7, 9, 8):
        frm = (z + d) % N_HEAD
        send(cgat.at[frm], cgat.at[frm], c_s.at[d], c_r.at[frm], head=frm).wait_recv()
        proj += mm(cgat[frm], weight_ref[block_rows(frm, 128), :])
    proj = proj * inv_len
    zown[...] = proj
    z_copy = send(zown, zprev, one_s.at[3], one_r.at[3], tm=nxt)
    z_copy.start()

    hi = proj.astype(BF16)
    zst[0:32, :] = hi
    zst[32:64, :] = (proj - hi.astype(F32)).astype(BF16)
    zst[64:128, :] = jnp.zeros((64, BLOCK), BF16)

    rows_z = [zst[...] * hm[h, 0:128, :] for h in range(NH)]
    back = mm(pull_all[0], rows_z[0])
    for h in range(1, NH):
        back += mm(pull_all[h], rows_z[h])
    for half in range(2):
        cut = slice(128 * half, 128 * half + 128)
        adj[half] = back[:, cut]
        adj_b[half] = back[:, cut].astype(BF16)
    adj_copy = send(adj_b, pair_a, one_s.at[6], one_r.at[6], tm=pair)
    adj_copy.start()

    def await_log(d, carry):
        frm = (chip + d) % CHIPS
        send(lgt.at[frm], lgt.at[frm], lg_s.at[frm], lg_r.at[frm], tm=frm * 2 + core).wait_recv()
        return carry

    lax.fori_loop(1, CHIPS, await_log, 0)

    def take_state(m, acc):
        send(tot_s, st_t.at[m], t_s.at[m], t_r.at[m], tm=m * 2 + core).wait_recv()
        return jnp.exp(lgt[m][0:1, :]) * acc + st_t[m].astype(F32)

    ent[core] = lax.fori_loop(0, chip, take_state, jnp.zeros((128, 128), F32))
    ent_copy = send(ent.at[core], ent.at[core], one_s.at[4], one_r.at[4 + core], tm=pair)
    ent_copy.start()

    adj_copy.wait_recv()
    mine = adj[core]
    other = pair_a[core].astype(F32)
    a0 = jnp.where(first, mine, other)
    a1 = jnp.where(first, other, mine)
    tot_a[...] = (a0 + jnp.exp(l0) * a1).astype(BF16)

    def send_adjoint(to, carry):
        send(tot_a, ad_t.at[chip], a_s.at[to], a_r.at[chip], tm=to * 2 + core).start()
        return carry

    lax.fori_loop(0, chip, send_adjoint, 0)

    send(ent.at[core], ent.at[1 - core], one_s.at[4], one_r.at[5 - core], tm=pair).wait_recv()
    halves = []
    for half in range(2):
        came = ent[half]
        halves.append(jnp.where(first, came, jnp.exp(log0[half]) * came + pair_s[half].astype(F32)))
    carry_state = jnp.concatenate(halves, axis=1)
    for b in range(NB):
        entry[b] = carry_state.astype(BF16)
        if b < NB - 1:
            carry_state = jnp.exp(totx[b, 0:1, :]) * carry_state + sblk[b]

    def hand_on(buf, mid, s, r, b):
        for k in range(4):
            to = b * 4 + k
            off = (to - z + N_HEAD) % N_HEAD

            @pl.when((off % 2 == 0) & (off > 0))
            def _():
                near = (z + 1 - 2 * (off // 9) + N_HEAD) % N_HEAD
                send(buf.at[to], mid.at[to], s.at[to], r.at[to], head=near).start()

    def send_sums(buf, mid, into, s, m, r):
        for off in (9, 7, 5, 11, 3, 13, 1, 15):
            to = (z + off) % N_HEAD
            if off != 9:
                send(buf.at[to], mid.at[to], s.at[to], m.at[to], head=to).wait_recv()
                buf[to] = (buf[to].astype(F32) + mid[to].astype(F32)).astype(BF16)
            send(buf.at[to], into.at[z], s.at[to], r.at[z], head=to).start()

    def local_adjoint(i, carry):
        b = NB - 1 - i
        rows = block_rows(b)
        g = mm(mask[rows, :], zst[...]).astype(BF16)
        gy[b] = g
        grown = (g.astype(F32) * growx[b]).astype(BF16)
        gg[b] = grown
        return carry

    def block_adjoint(i, carry):
        b = NB - 1 - i
        ablk[b] = mm_tn(read_ref[block_rows(b), :], gg[b])
        return carry

    def local_cross(i, carry):
        b = NB - 1 - i
        rows = block_rows(b)
        g = gy[b]
        xb = x_ref[rows, :]
        both = jnp.zeros((BLOCK, BLOCK), F32)
        for h in range(NH):
            both += decay[b * NH + h] * mm_nt(g * hm[h], xb)
        both = both.astype(BF16)
        part = mm(both, write_ref[rows, :]) + mm_nt(gg[b], entry[b])
        for k in range(4):
            rs_r[b * 4 + k] = part[64 * k : 64 * k + 64, :].astype(BF16)
        hand_on(rs_r, mid_r, rr_s, mid_r_s, b)
        wr_acc[b] = mm_tn(both, read_ref[rows, :])
        return carry

    def cotangent_and_cross(i, carry):
        return local_cross(i, local_adjoint(i, carry))

    lax.fori_loop(0, NB - 1, cotangent_and_cross, 0)
    z_copy.wait_recv()
    before = zprev[...]
    hi = before.astype(BF16)
    zst[64:96, :] = hi
    zst[96:128, :] = (before - hi.astype(F32)).astype(BF16)
    lax.fori_loop(NB - 1, NB, cotangent_and_cross, 0)

    def pooled(b, acc):
        rows = block_rows(b)
        y = (out_acc[b] + growx[b] * mm(read_ref[rows, :], entry[b])).astype(BF16)
        return acc + mm_tn(mask[rows, :], y)

    pool = pooled(0, jnp.zeros((128, BLOCK), F32))
    ppart[...] = pool[64:96, :]
    p_copy = send(ppart, pprev, one_s.at[7], one_r.at[7], tm=prv)
    p_copy.start()

    pool = lax.fori_loop(1, NB, pooled, pool)
    lax.fori_loop(0, NB - 1, block_adjoint, 0)
    spilt = mm(pull_next[0], rows_z[0])
    for h in range(1, NH):
        spilt += mm(pull_next[h], rows_z[h])
    spill_adj[...] = spilt

    cols[me] = cgat[chip]

    def send_cols(d, carry):
        to = (me + d) % N_TM
        send(cgat.at[to // 2], cols.at[me], cols_s.at[to], cols_r.at[me], tm=to).start()
        return carry

    lax.fori_loop(1, N_TM, send_cols, 0)


    send_sums(rs_r, mid_r, rr, rr_s, mid_r_s, rr_r)

    def send_pool(d, carry):
        to = (me + d) % N_TM
        send(plb.at[me], plb.at[me], pl_s.at[to], pl_r.at[me], tm=to).start()
        return carry

    def take_adjoint(i, acc):
        m = CHIPS - 1 - i
        send(tot_a, ad_t.at[m], a_s.at[m], a_r.at[m], tm=m * 2 + core).wait_recv()
        return jnp.exp(lgt[m][0:1, :]) * acc + ad_t[m].astype(F32)

    ext[core] = lax.fori_loop(0, CHIPS - 1 - chip, take_adjoint, jnp.zeros((128, 128), F32))
    ext_copy = send(ext.at[core], ext.at[core], one_s.at[8], one_r.at[8 + core], tm=pair)
    ext_copy.start()
    p_copy.wait_recv()
    plb[me] = ((pool[0:32, :] + pprev[...]) * inv_len).astype(BF16)
    lax.fori_loop(1, N_TM, send_pool, 0)
    send(ext.at[core], ext.at[1 - core], one_s.at[8], one_r.at[9 - core], tm=pair).wait_recv()
    halves = []
    for half in range(2):
        came = ext[half]
        halves.append(jnp.where(first, jnp.exp(log1[half]) * came + pair_a[half].astype(F32), came))
    carry_adj = jnp.concatenate(halves, axis=1) + spill_adj[...]
    for b in range(NB - 1, -1, -1):
        leave[b] = carry_adj.astype(BF16)
        if b > 0:
            carry_adj = jnp.exp(totx[b, 0:1, :]) * carry_adj + ablk[b]

    def late_write(i, carry):
        b = i
        part = wr_acc[b] + mm_nt(xf[b], leave[b])
        for k in range(4):
            rs_w[b * 4 + k] = part[64 * k : 64 * k + 64, :].astype(BF16)
        hand_on(rs_w, mid_w, rw_s, mid_w_s, b)
        return carry

    lax.fori_loop(0, NB, late_write, 0)

    def late_inputs(b, carry):
        rows = block_rows(b)
        g = gy[b]
        into = fadex[b] * mm(write_ref[rows, :], leave[b])
        for h in range(NH):
            into += mm_tn(scores[b * NH + h], g * hm[h])
        gi_vm[rows, :] = into.astype(BF16)
        return carry

    lax.fori_loop(0, 2, late_inputs, 0)
    send_sums(rs_w, mid_w, rw, rw_s, mid_w_s, rw_r)
    lax.fori_loop(2, NB, late_inputs, 0)
    gi_copy = pltpu.make_async_copy(gi_vm, gi_ref, in_s.at[8])
    gi_copy.start()

    def await_pool(d, carry):
        frm = (me + d) % N_TM
        send(cgat.at[0], cols.at[frm], cols_s.at[frm], cols_r.at[frm], tm=frm).wait_recv()
        send(plb.at[frm], plb.at[frm], pl_s.at[frm], pl_r.at[frm], tm=frm).wait_recv()
        return carry

    lax.fori_loop(1, N_TM, await_pool, 0)
    weight_grad = mm_tn(cols[...].reshape(N_TM * CAP, 128), plb[...].reshape(N_TM * CAP, BLOCK))
    gow_vm[...] = jnp.where(first, weight_grad[0:64, :], weight_grad[64:128, :])
    gow_copy = pltpu.make_async_copy(gow_vm, gow_ref, in_s.at[9])
    gow_copy.start()

    def take(buf, into, s, r):
        def step(i, acc):
            frm = (z + 2 * i + 1) % N_HEAD
            send(buf.at[frm], into.at[frm], s.at[frm], r.at[frm], head=frm).wait_recv()
            return acc + into[frm].astype(F32)

        return lax.fori_loop(0, N_HEAD // 2, step, buf[z].astype(F32))

    gr_vm[...] = take(rs_r, rr, rr_s, rr_r)
    gr_copy = pltpu.make_async_copy(gr_vm, gr_ref, in_s.at[10])
    gr_copy.start()

    for d in range(1, N_HEAD):
        send(cgat.at[z], cgat.at[z], c_s.at[d], c_r.at[z], head=(z + d) % N_HEAD).wait_send()
    for copy in (meta_copy, rows_copy, run_copy, state_copy, lg_copy, z_copy, ent_copy, adj_copy, p_copy, ext_copy):
        copy.wait_send()

    def sent_tm(d, carry):
        to = (me + d) % N_TM
        send(cgat.at[0], cols.at[me], cols_s.at[to], cols_r.at[me], tm=to).wait_send()
        send(plb.at[me], plb.at[me], pl_s.at[to], pl_r.at[me], tm=to).wait_send()
        return carry

    def sent_log(d, carry):
        to = (chip + d) % CHIPS
        send(lgt.at[chip], lgt.at[chip], lg_s.at[to], lg_r.at[chip], tm=to * 2 + core).wait_send()
        return carry

    def sent_state(to, carry):
        send(tot_s, st_t.at[chip], t_s.at[to], t_r.at[chip], tm=to * 2 + core).wait_send()
        return carry

    def sent_adjoint(to, carry):
        send(tot_a, ad_t.at[chip], a_s.at[to], a_r.at[chip], tm=to * 2 + core).wait_send()
        return carry

    lax.fori_loop(1, N_TM, sent_tm, 0)
    lax.fori_loop(1, CHIPS, sent_log, 0)
    lax.fori_loop(chip + 1, CHIPS, sent_state, 0)
    lax.fori_loop(0, chip, sent_adjoint, 0)

    gw_vm[...] = take(rs_w, rw, rw_s, rw_r)
    gw_copy = pltpu.make_async_copy(gw_vm, gw_ref, in_s.at[11])
    gw_copy.start()

    def sent_head(d, carry):
        to = (z + d) % N_HEAD
        send(rs_r.at[to], rr.at[z], rr_s.at[to], rr_r.at[z], head=to).wait_send()
        send(rs_w.at[to], rw.at[z], rw_s.at[to], rw_r.at[z], head=to).wait_send()
        return carry

    lax.fori_loop(1, N_HEAD, sent_head, 0)
    for copy in (gi_copy, gow_copy, gr_copy, gw_copy):
        copy.wait()


def write_out(gi, gw, gr, gow, gi_out, gw_out, gr_out, gow_out, gi_vm, gw_vm, gr_vm, gow_vm, came, left):
    size = gi.shape[0] // 4
    moves = [(gi.at[pl.ds(i * size, size)], gi_vm.at[pl.ds(i * size, size)], gi_out.at[pl.ds(i * size, size)]) for i in range(4)]
    moves += [(gw, gw_vm, gw_out), (gr, gr_vm, gr_out), (gow, gow_vm, gow_out)]
    ins = [pltpu.make_async_copy(a, b, came.at[i]) for i, (a, b, _) in enumerate(moves)]
    outs = [pltpu.make_async_copy(b, c, left.at[i]) for i, (_, b, c) in enumerate(moves)]
    for copy in ins:
        copy.start()
    for here, there in zip(ins, outs):
        here.wait()
        there.start()
    for copy in outs:
        copy.wait()


def body(frame_inputs, write_map, read_map, log_decay, out_weight, caption_grad, caption_start, caption_end):
    frames, width = frame_inputs.shape
    V = pltpu.VMEM
    DMA = pltpu.SemaphoreType.DMA
    state = (2, 128, 128)
    tile = (BLOCK, BLOCK)
    scratch = [
        V(frame_inputs.shape, BF16),
        V(write_map.shape, BF16),
        V(read_map.shape, BF16),
        V(log_decay.shape, F32),
        V(out_weight.shape, BF16),
        V(caption_grad.shape, F32),
        V((1, CAP), jnp.int32),
        V((1, CAP), jnp.int32),
        DMA((12,)),
        V((N_HEAD, CAP, 128), BF16),
        V((N_TM, CAP, 128), BF16),
        V((2, 8, 128), F32),
        V((2, 8, 128), F32),
        V((CAP, BLOCK), F32),
        V((CAP, BLOCK), F32),
        V((128, BLOCK), BF16),
        V((frames, 128), BF16),
        V((NH, *tile), BF16),
        V((8, frames), F32),
        V((NB, 8, BLOCK), F32),
        V((NB, *tile), F32),
        V((NB, *tile), F32),
        V((NB, 8, BLOCK), F32),
        V((NB, *tile), BF16),
        V((NB, *tile), BF16),
        V((NB, *tile), BF16),
        V((NB, 128, BLOCK), F32),
        V((NB, 128, BLOCK), F32),
        V((NB * NH, *tile), F32),
        V((NB * NH, *tile), BF16),
        V((NB, *tile), F32),
        V((NB, BLOCK, 128), F32),
        V((NB, 128, BLOCK), BF16),
        V((NB, 128, BLOCK), BF16),
        V(state, F32),
        V(state, BF16),
        V(state, BF16),
        V(state, BF16),
        V(state, F32),
        V(state, BF16),
        V((2, 8, 128), F32),
        V((2, 8, 128), F32),
        V((CHIPS, 8, 128), F32),
        V((CHIPS, 128, 128), BF16),
        V((CHIPS, 128, 128), BF16),
        V((128, 128), BF16),
        V((128, 128), BF16),
        V(state, F32),
        V(state, F32),
        V((BLOCK, 128), BF16),
        V((8, BLOCK), F32),
        V((NH, 128, 128), F32),
        V((NH, 128, 128), BF16),
        V((NH, 128, 128), BF16),
        V((BLOCK, 128), BF16),
        V((128, BLOCK), F32),
        V((CAP, BLOCK), F32),
        V((CAP, BLOCK), F32),
        V((N_TM, CAP, BLOCK), BF16),
        V((N_HEAD, 64, 128), BF16),
        V((N_HEAD, 64, 128), BF16),
        V((N_HEAD, 64, 128), BF16),
        V((N_HEAD, 64, 128), BF16),
        V((N_HEAD, 64, 128), BF16),
        V((N_HEAD, 64, 128), BF16),
        V(frame_inputs.shape, BF16),
        V((64, 128), F32),
        V((64, 128), F32),
        V((64, BLOCK), F32),
        DMA((N_HEAD,)),
        DMA((N_HEAD,)),
        DMA((N_TM,)),
        DMA((N_TM,)),
        DMA((12,)),
        DMA((12,)),
        DMA((CHIPS,)),
        DMA((CHIPS,)),
        DMA((CHIPS,)),
        DMA((CHIPS,)),
        DMA((CHIPS,)),
        DMA((CHIPS,)),
        DMA((N_TM,)),
        DMA((N_TM,)),
        DMA((N_HEAD,)),
        DMA((N_HEAD,)),
        DMA((N_HEAD,)),
        DMA((N_HEAD,)),
        DMA((N_HEAD,)),
        DMA((N_HEAD,)),
    ]
    results = pl.pallas_call(
        kernel,
        out_shape=(
            jax.ShapeDtypeStruct((frames, width), BF16),
            jax.ShapeDtypeStruct((64, 128), F32),
            jax.ShapeDtypeStruct((64, 128), F32),
            jax.ShapeDtypeStruct((64, BLOCK), F32),
        ),
        in_specs=[pl.BlockSpec(memory_space=pltpu.HBM)] * 8,
        out_specs=(pl.BlockSpec(memory_space=pltpu.HBM),) * 4,
        scratch_shapes=scratch,
        compiler_params=pltpu.CompilerParams(
            collective_id=0, has_side_effects=True, vmem_limit_bytes=63 * 1024 * 1024
        ),
    )(
        frame_inputs, write_map, read_map, log_decay, out_weight, caption_grad,
        caption_start.reshape(1, CAP), caption_end.reshape(1, CAP),
    )
    return pl.pallas_call(
        write_out,
        out_shape=tuple(jax.ShapeDtypeStruct(r.shape, r.dtype) for r in results),
        in_specs=[pl.BlockSpec(memory_space=pltpu.HBM)] * 4,
        out_specs=(pl.BlockSpec(memory_space=pltpu.HBM),) * 4,
        scratch_shapes=[V(r.shape, r.dtype) for r in results] + [DMA((7,)), DMA((7,))],
        compiler_params=pltpu.CompilerParams(vmem_limit_bytes=62 * 1024 * 1024),
    )(*results)


def solution(mesh):
    in_specs = (
        P("tm", "head"),
        P("tm", None),
        P("tm", None),
        P("head", "tm"),
        P(None, "head"),
        P("tm", "head"),
        P("tm"),
        P("tm"),
    )
    out_specs = (P("tm", "head"), P(("tm", "head"), None), P(("tm", "head"), None), P("tm", "head"))
    return jax.shard_map(body, mesh=mesh, in_specs=in_specs, out_specs=out_specs, check_vma=False)
```

```python
import jax
import jax.numpy as jnp
from jax import lax
from jax.experimental import pallas as pl
from jax.experimental.pallas import tpu as pltpu
from jax.sharding import PartitionSpec as P

BLOCK = 256
F32 = jnp.float32
BF16 = jnp.bfloat16
MESH = pl.DeviceIdType.MESH
HIGH = lax.Precision.HIGHEST
N_TM = 32
N_HEAD = 16
CHIPS = N_TM // 2
NB = 4
NH = 4
CAP = 32
FAR_FIRST = (8, 7, 9, 6, 10, 5, 11, 4, 12, 3, 13, 2, 14, 1, 15)


def mm(a, b):
    return lax.dot_general(a, b, (((1,), (0,)), ((), ())), preferred_element_type=F32)


def mm_nt(a, b):
    return lax.dot_general(a, b, (((1,), (1,)), ((), ())), preferred_element_type=F32)


def mm_tn(a, b):
    return lax.dot_general(a, b, (((0,), (0,)), ((), ())), preferred_element_type=F32)


def block_rows(b, size=BLOCK):
    return pl.ds(pl.multiple_of(b * size, size), size)


def kernel(
    x_hbm, write_hbm, read_hbm, decay_hbm, weight_hbm, cap_hbm, start_hbm, end_hbm,
    gi_ref, gw_ref, gr_ref, gow_ref,
    x_ref, write_ref, read_ref, decay_ref, weight_ref, cap_ref, start_ref, end_ref, in_s,
    cgat, cols, meta, meta_prev, zown, zprev, zst, mask, hm,
    ld8, rowrun, growx, fadex, totx, xf, gg, gy, sblk, ablk, decay, scores,
    out_acc, wr_acc, entry, leave,
    dev, dev_b, pair_s, pair_a, adj, adj_b, lg, lg_pair, lgt, st_t, ad_t, tot_s, tot_a, ent, ext,
    next_read, next_run, pull, pull_next, pull_all, spill, spill_adj,
    ppart, pprev, plb, rs_r, rs_w, mid_r, mid_w, rr, rw, gi_vm, gw_vm, gr_vm, gow_vm,
    c_s, c_r, cols_s, cols_r, one_s, one_r, lg_s, lg_r, t_s, t_r, a_s, a_r, pl_s, pl_r, rr_s, rr_r, rw_s, rw_r, mid_r_s, mid_w_s,
):
    me = lax.axis_index("tm")
    z = lax.axis_index("head")
    chip = me // 2
    core = me % 2
    pair = me + 1 - 2 * core
    nxt = (me + 1) % N_TM
    prv = (me + N_TM - 1) % N_TM

    def send(src, dst, s, r, **where):
        return pltpu.make_async_remote_copy(
            src_ref=src, dst_ref=dst, send_sem=s, recv_sem=r, device_id=where, device_id_type=MESH
        )

    fetch = [
        pltpu.make_async_copy(src, dst, in_s.at[i])
        for i, (src, dst) in enumerate(
            (
                (cap_hbm, cap_ref),
                (start_hbm, start_ref),
                (end_hbm, end_ref),
                (decay_hbm, decay_ref),
                (x_hbm, x_ref),
                (write_hbm, write_ref),
                (read_hbm, read_ref),
                (weight_hbm, weight_ref),
            )
        )
    ]
    for copy in fetch[:7]:
        copy.start()
    barrier = pltpu.get_barrier_semaphore()

    def hail_tm(d, carry):
        pl.semaphore_signal(barrier, inc=1, device_id={"tm": (me + d) % N_TM}, device_id_type=MESH)
        return carry

    def hail_head(d, carry):
        pl.semaphore_signal(barrier, inc=1, device_id={"head": (z + d) % N_HEAD}, device_id_type=MESH)
        return carry

    for d in FAR_FIRST:
        hail_head(d, 0)
    lax.fori_loop(1, N_TM, hail_tm, 0)

    lane_head = lax.broadcasted_iota(jnp.int32, (BLOCK, BLOCK), 1) // 64
    row_id = lax.broadcasted_iota(jnp.int32, (BLOCK, BLOCK), 0)
    col_id = lax.broadcasted_iota(jnp.int32, (BLOCK, BLOCK), 1)
    for h in range(NH):
        hm[h] = (lane_head == h).astype(F32).astype(BF16)
    tri = (row_id <= col_id).astype(F32).astype(BF16)
    ld8[...] = jnp.zeros_like(ld8)
    fetch[3].wait()
    ld8[0:4, :] = decay_ref[...]
    fetch[4].wait()
    fetch[5].wait()

    def local_state(b, carry):
        rows = block_rows(b)
        left = ld8[:, rows]
        run = jnp.zeros((8, BLOCK), F32)
        for _ in range(3):
            part = left.astype(BF16)
            run += mm(part, tri)
            left = left - part.astype(F32)
        rowrun[b] = run
        col = run.T
        runx = jnp.where(
            lane_head < 2,
            jnp.where(lane_head < 1, col[:, 0:1], col[:, 1:2]),
            jnp.where(lane_head < 3, col[:, 2:3], col[:, 3:4]),
        )
        total = runx[BLOCK - 1 : BLOCK, :]
        growx[b] = jnp.exp(runx)
        fade = jnp.exp(total - runx)
        fadex[b] = fade
        totx[b] = jnp.broadcast_to(total, (8, BLOCK))
        faded = (x_ref[rows, :].astype(F32) * fade).astype(BF16)
        xf[b] = faded
        sblk[b] = mm_tn(write_ref[rows, :], faded)
        return carry

    lax.fori_loop(0, NB, local_state, 0)

    state = sblk[0]
    for b in range(1, NB):
        state = jnp.exp(totx[b, 0:1, :]) * state + sblk[b]
    log_all = totx[0] + totx[1] + totx[2] + totx[3]
    for half in range(2):
        cut = slice(128 * half, 128 * half + 128)
        dev[half] = state[:, cut]
        dev_b[half] = state[:, cut].astype(BF16)
        lg[half] = log_all[:, cut]

    fetch[0].wait()
    cgat[z] = cap_ref[...].astype(BF16)

    pl.semaphore_wait(barrier, N_TM - 1 + N_HEAD - 1)
    for d in FAR_FIRST:
        send(cgat.at[z], cgat.at[z], c_s.at[d], c_r.at[z], head=(z + d) % N_HEAD).start()
    state_copy = send(dev_b, pair_s, one_s.at[1], one_r.at[1], tm=pair)
    state_copy.start()
    lg_copy = send(lg, lg_pair, one_s.at[2], one_r.at[2], tm=pair)
    lg_copy.start()
    fetch[7].start()
    fetch[6].wait()
    rows_copy = send(read_ref.at[pl.ds(0, BLOCK)], next_read, one_s.at[5], one_r.at[10], tm=prv)
    rows_copy.start()
    run_copy = send(rowrun.at[0], next_run, one_s.at[9], one_r.at[11], tm=prv)
    run_copy.start()

    fetch[1].wait()
    fetch[2].wait()
    spread = (
        lax.broadcasted_iota(jnp.int32, (CAP, 128), 1) % CAP
        == lax.broadcasted_iota(jnp.int32, (CAP, 128), 0)
    ).astype(F32)
    start_f = start_ref[...].astype(F32)
    end_f = end_ref[...].astype(F32)
    start_row = jnp.dot(jnp.broadcast_to(start_f, (8, CAP)), spread, precision=HIGH, preferred_element_type=F32)
    end_row = jnp.dot(jnp.broadcast_to(end_f, (8, CAP)), spread, precision=HIGH, preferred_element_type=F32)
    meta[0] = start_row
    meta[1] = end_row
    eye = lax.broadcasted_iota(jnp.int32, (CAP, CAP), 0) == lax.broadcasted_iota(jnp.int32, (CAP, CAP), 1)
    inv_len = jnp.sum(jnp.where(eye, 1.0 / jnp.maximum(end_f - start_f, 1.0), 0.0), axis=1, keepdims=True)

    meta_copy = send(meta, meta_prev, one_s.at[0], one_r.at[0], tm=nxt)
    meta_copy.start()

    def local_scores(b, carry):
        rows = block_rows(b)
        both = mm_nt(read_ref[rows, :], write_ref[rows, :])
        run = rowrun[b]
        col = run.T
        xb = x_ref[rows, :]
        out = jnp.zeros((BLOCK, BLOCK), F32)
        for h in range(NH):
            gap = col[:, h : h + 1] - run[h : h + 1, :]
            dec = jnp.exp(jnp.where(row_id >= col_id, gap, -jnp.inf))
            decay[b * NH + h] = dec
            sc = (both * dec).astype(BF16)
            scores[b * NH + h] = sc
            out += mm(sc, xb * hm[h])
        out_acc[b] = out
        return carry

    lax.fori_loop(0, 2, local_scores, 0)

    state_copy.wait_recv()
    lg_copy.wait_recv()
    first = core == 0
    log0 = [jnp.where(first, lg[h], lg_pair[h])[0:1, :] for h in range(2)]
    log1 = [jnp.where(first, lg_pair[h], lg[h])[0:1, :] for h in range(2)]

    mine = dev[core]
    other = pair_s[core].astype(F32)
    s0 = jnp.where(first, mine, other)
    s1 = jnp.where(first, other, mine)
    l0 = jnp.where(first, log0[0], log0[1])
    l1 = jnp.where(first, log1[0], log1[1])
    tot_s[...] = (s1 + jnp.exp(l1) * s0).astype(BF16)
    lgt[chip] = jnp.broadcast_to(l0 + l1, (8, 128))

    def send_log(d, carry):
        to = (chip + d) % CHIPS
        send(lgt.at[chip], lgt.at[chip], lg_s.at[to], lg_r.at[chip], tm=to * 2 + core).start()
        return carry

    def send_state(to, carry):
        send(tot_s, st_t.at[chip], t_s.at[to], t_r.at[chip], tm=to * 2 + core).start()
        return carry

    lax.fori_loop(1, CHIPS, send_log, 0)
    lax.fori_loop(chip + 1, CHIPS, send_state, 0)
    lax.fori_loop(2, NB, local_scores, 0)

    meta_copy.wait_recv()
    lane = lax.broadcasted_iota(jnp.int32, (BLOCK, 128), 1)
    frame = lax.broadcasted_iota(jnp.int32, (BLOCK, 128), 0)
    seg_start = jnp.where(lane[0:8] < 64, meta[0], meta_prev[0])[0:1, :]
    seg_end = jnp.where(lane[0:8] < 64, meta[1], meta_prev[1])[0:1, :]

    def cover(b, carry):
        t = (frame + (me * (NB * BLOCK) + b * BLOCK)).astype(F32)
        inside = jnp.where(t >= seg_start, jnp.where(t < seg_end, 1.0, 0.0), 0.0)
        mask[block_rows(b), :] = inside.astype(BF16)
        return carry

    lax.fori_loop(0, NB, cover, 0)

    t = (frame + (me + 1) * (NB * BLOCK)).astype(F32)
    inside = jnp.where(t >= seg_start, jnp.where(t < seg_end, 1.0, 0.0), 0.0)
    spill[...] = jnp.where(lane < 64, inside, 0.0).astype(BF16)
    rows_copy.wait_recv()
    run_copy.wait_recv()
    col = next_run[...].T
    growth_next = jnp.exp(
        jnp.where(
            lane_head < 2,
            jnp.where(lane_head < 1, col[:, 0:1], col[:, 1:2]),
            jnp.where(lane_head < 3, col[:, 2:3], col[:, 3:4]),
        )
    )

    for h in range(NH):
        pull[h] = jnp.zeros((128, 128), F32)

    def local_pull(i, carry):
        b = NB - 1 - i
        rows = block_rows(b)
        grown = growx[b]
        total = totx[b, 0:1, :]
        reads = read_ref[rows, :].astype(F32)
        for h in range(NH):
            one = slice(64 * h, 64 * h + 1)
            scaled = (reads * grown[:, one]).astype(BF16)
            pull[h] = jnp.exp(total[:, one]) * pull[h] + mm_tn(scaled, mask[rows, :])
        return carry

    lax.fori_loop(0, NB, local_pull, 0)
    dev_log = totx[0, 0:1, :] + totx[1, 0:1, :] + totx[2, 0:1, :] + totx[3, 0:1, :]
    reads = next_read[...].astype(F32)
    for h in range(NH):
        one = slice(64 * h, 64 * h + 1)
        scaled = (reads * growth_next[:, one]).astype(BF16)
        part = mm_tn(scaled, spill[...])
        pull_next[h] = part.astype(BF16)
        pull_all[h] = (pull[h] + jnp.exp(dev_log[:, one]) * part).astype(BF16)

    fetch[7].wait()
    proj = mm(cgat[z], weight_ref[block_rows(z, 128), :])
    for d in (1, 15, 2, 14, 3, 13, 4, 12, 5, 11, 6, 10, 7, 9, 8):
        frm = (z + d) % N_HEAD
        send(cgat.at[frm], cgat.at[frm], c_s.at[d], c_r.at[frm], head=frm).wait_recv()
        proj += mm(cgat[frm], weight_ref[block_rows(frm, 128), :])
    proj = proj * inv_len
    zown[...] = proj
    z_copy = send(zown, zprev, one_s.at[3], one_r.at[3], tm=nxt)
    z_copy.start()

    hi = proj.astype(BF16)
    zst[0:32, :] = hi
    zst[32:64, :] = (proj - hi.astype(F32)).astype(BF16)
    zst[64:128, :] = jnp.zeros((64, BLOCK), BF16)

    rows_z = [zst[...] * hm[h, 0:128, :] for h in range(NH)]
    back = mm(pull_all[0], rows_z[0])
    for h in range(1, NH):
        back += mm(pull_all[h], rows_z[h])
    for half in range(2):
        cut = slice(128 * half, 128 * half + 128)
        adj[half] = back[:, cut]
        adj_b[half] = back[:, cut].astype(BF16)
    adj_copy = send(adj_b, pair_a, one_s.at[6], one_r.at[6], tm=pair)
    adj_copy.start()

    def await_log(d, carry):
        frm = (chip + d) % CHIPS
        send(lgt.at[frm], lgt.at[frm], lg_s.at[frm], lg_r.at[frm], tm=frm * 2 + core).wait_recv()
        return carry

    lax.fori_loop(1, CHIPS, await_log, 0)

    def take_state(m, acc):
        send(tot_s, st_t.at[m], t_s.at[m], t_r.at[m], tm=m * 2 + core).wait_recv()
        return jnp.exp(lgt[m][0:1, :]) * acc + st_t[m].astype(F32)

    ent[core] = lax.fori_loop(0, chip, take_state, jnp.zeros((128, 128), F32))
    ent_copy = send(ent.at[core], ent.at[core], one_s.at[4], one_r.at[4 + core], tm=pair)
    ent_copy.start()

    adj_copy.wait_recv()
    mine = adj[core]
    other = pair_a[core].astype(F32)
    a0 = jnp.where(first, mine, other)
    a1 = jnp.where(first, other, mine)
    tot_a[...] = (a0 + jnp.exp(l0) * a1).astype(BF16)

    def send_adjoint(to, carry):
        send(tot_a, ad_t.at[chip], a_s.at[to], a_r.at[chip], tm=to * 2 + core).start()
        return carry

    lax.fori_loop(0, chip, send_adjoint, 0)

    send(ent.at[core], ent.at[1 - core], one_s.at[4], one_r.at[5 - core], tm=pair).wait_recv()
    halves = []
    for half in range(2):
        came = ent[half]
        halves.append(jnp.where(first, came, jnp.exp(log0[half]) * came + pair_s[half].astype(F32)))
    carry_state = jnp.concatenate(halves, axis=1)
    for b in range(NB):
        entry[b] = carry_state.astype(BF16)
        if b < NB - 1:
            carry_state = jnp.exp(totx[b, 0:1, :]) * carry_state + sblk[b]

    def hand_on(buf, mid, s, r, b):
        for k in range(4):
            to = b * 4 + k
            off = (to - z + N_HEAD) % N_HEAD

            @pl.when((off % 2 == 0) & (off > 0))
            def _():
                near = (z + 1 - 2 * (off // 9) + N_HEAD) % N_HEAD
                send(buf.at[to], mid.at[to], s.at[to], r.at[to], head=near).start()

    def send_sums(buf, mid, into, s, m, r):
        for off in (9, 7, 5, 11, 3, 13, 1, 15):
            to = (z + off) % N_HEAD
            if off != 9:
                send(buf.at[to], mid.at[to], s.at[to], m.at[to], head=to).wait_recv()
                buf[to] = (buf[to].astype(F32) + mid[to].astype(F32)).astype(BF16)
            send(buf.at[to], into.at[z], s.at[to], r.at[z], head=to).start()

    def local_adjoint(i, carry):
        b = NB - 1 - i
        rows = block_rows(b)
        g = mm(mask[rows, :], zst[...]).astype(BF16)
        gy[b] = g
        grown = (g.astype(F32) * growx[b]).astype(BF16)
        gg[b] = grown
        return carry

    def block_adjoint(i, carry):
        b = NB - 1 - i
        ablk[b] = mm_tn(read_ref[block_rows(b), :], gg[b])
        return carry

    def local_cross(i, carry):
        b = NB - 1 - i
        rows = block_rows(b)
        g = gy[b]
        xb = x_ref[rows, :]
        both = jnp.zeros((BLOCK, BLOCK), F32)
        for h in range(NH):
            both += decay[b * NH + h] * mm_nt(g * hm[h], xb)
        both = both.astype(BF16)
        part = mm(both, write_ref[rows, :]) + mm_nt(gg[b], entry[b])
        for k in range(4):
            rs_r[b * 4 + k] = part[64 * k : 64 * k + 64, :].astype(BF16)
        hand_on(rs_r, mid_r, rr_s, mid_r_s, b)
        wr_acc[b] = mm_tn(both, read_ref[rows, :])
        return carry

    def cotangent_and_cross(i, carry):
        return local_cross(i, local_adjoint(i, carry))

    lax.fori_loop(0, NB - 1, cotangent_and_cross, 0)
    z_copy.wait_recv()
    before = zprev[...]
    hi = before.astype(BF16)
    zst[64:96, :] = hi
    zst[96:128, :] = (before - hi.astype(F32)).astype(BF16)
    lax.fori_loop(NB - 1, NB, cotangent_and_cross, 0)

    def pooled(b, acc):
        rows = block_rows(b)
        y = (out_acc[b] + growx[b] * mm(read_ref[rows, :], entry[b])).astype(BF16)
        return acc + mm_tn(mask[rows, :], y)

    pool = pooled(0, jnp.zeros((128, BLOCK), F32))
    ppart[...] = pool[64:96, :]
    p_copy = send(ppart, pprev, one_s.at[7], one_r.at[7], tm=prv)
    p_copy.start()

    pool = lax.fori_loop(1, NB, pooled, pool)
    lax.fori_loop(0, NB - 1, block_adjoint, 0)
    spilt = mm(pull_next[0], rows_z[0])
    for h in range(1, NH):
        spilt += mm(pull_next[h], rows_z[h])
    spill_adj[...] = spilt

    send_sums(rs_r, mid_r, rr, rr_s, mid_r_s, rr_r)

    def send_pool(d, carry):
        to = (me + d) % N_TM
        send(plb.at[me], plb.at[me], pl_s.at[to], pl_r.at[me], tm=to).start()
        return carry

    def take_adjoint(i, acc):
        m = CHIPS - 1 - i
        send(tot_a, ad_t.at[m], a_s.at[m], a_r.at[m], tm=m * 2 + core).wait_recv()
        return jnp.exp(lgt[m][0:1, :]) * acc + ad_t[m].astype(F32)

    ext[core] = lax.fori_loop(0, CHIPS - 1 - chip, take_adjoint, jnp.zeros((128, 128), F32))
    ext_copy = send(ext.at[core], ext.at[core], one_s.at[8], one_r.at[8 + core], tm=pair)
    ext_copy.start()
    p_copy.wait_recv()
    plb[me] = ((pool[0:32, :] + pprev[...]) * inv_len).astype(BF16)
    lax.fori_loop(1, N_TM, send_pool, 0)
    send(ext.at[core], ext.at[1 - core], one_s.at[8], one_r.at[9 - core], tm=pair).wait_recv()
    halves = []
    for half in range(2):
        came = ext[half]
        halves.append(jnp.where(first, jnp.exp(log1[half]) * came + pair_a[half].astype(F32), came))
    carry_adj = jnp.concatenate(halves, axis=1) + spill_adj[...]
    for b in range(NB - 1, -1, -1):
        leave[b] = carry_adj.astype(BF16)
        if b > 0:
            carry_adj = jnp.exp(totx[b, 0:1, :]) * carry_adj + ablk[b]

    def late_write(i, carry):
        b = i
        part = wr_acc[b] + mm_nt(xf[b], leave[b])
        for k in range(4):
            rs_w[b * 4 + k] = part[64 * k : 64 * k + 64, :].astype(BF16)
        hand_on(rs_w, mid_w, rw_s, mid_w_s, b)
        return carry

    lax.fori_loop(0, NB, late_write, 0)

    cols[me] = cgat[chip]

    def send_cols(d, carry):
        to = (me + d) % N_TM
        send(cgat.at[to // 2], cols.at[me], cols_s.at[to], cols_r.at[me], tm=to).start()
        return carry

    lax.fori_loop(1, N_TM, send_cols, 0)


    def late_inputs(b, carry):
        rows = block_rows(b)
        g = gy[b]
        into = fadex[b] * mm(write_ref[rows, :], leave[b])
        for h in range(NH):
            into += mm_tn(scores[b * NH + h], g * hm[h])
        gi_vm[rows, :] = into.astype(BF16)
        return carry

    lax.fori_loop(0, 2, late_inputs, 0)
    send_sums(rs_w, mid_w, rw, rw_s, mid_w_s, rw_r)
    lax.fori_loop(2, NB, late_inputs, 0)
    gi_copy = pltpu.make_async_copy(gi_vm, gi_ref, in_s.at[8])
    gi_copy.start()

    def await_pool(d, carry):
        frm = (me + d) % N_TM
        send(cgat.at[0], cols.at[frm], cols_s.at[frm], cols_r.at[frm], tm=frm).wait_recv()
        send(plb.at[frm], plb.at[frm], pl_s.at[frm], pl_r.at[frm], tm=frm).wait_recv()
        return carry

    lax.fori_loop(1, N_TM, await_pool, 0)
    weight_grad = mm_tn(cols[...].reshape(N_TM * CAP, 128), plb[...].reshape(N_TM * CAP, BLOCK))
    gow_vm[...] = jnp.where(first, weight_grad[0:64, :], weight_grad[64:128, :])
    gow_copy = pltpu.make_async_copy(gow_vm, gow_ref, in_s.at[9])
    gow_copy.start()

    def take(buf, into, s, r):
        def step(i, acc):
            frm = (z + 2 * i + 1) % N_HEAD
            send(buf.at[frm], into.at[frm], s.at[frm], r.at[frm], head=frm).wait_recv()
            return acc + into[frm].astype(F32)

        return lax.fori_loop(0, N_HEAD // 2, step, buf[z].astype(F32))

    gr_vm[...] = take(rs_r, rr, rr_s, rr_r)
    gr_copy = pltpu.make_async_copy(gr_vm, gr_ref, in_s.at[10])
    gr_copy.start()

    for d in range(1, N_HEAD):
        send(cgat.at[z], cgat.at[z], c_s.at[d], c_r.at[z], head=(z + d) % N_HEAD).wait_send()
    for copy in (meta_copy, rows_copy, run_copy, state_copy, lg_copy, z_copy, ent_copy, adj_copy, p_copy, ext_copy):
        copy.wait_send()

    def sent_tm(d, carry):
        to = (me + d) % N_TM
        send(cgat.at[0], cols.at[me], cols_s.at[to], cols_r.at[me], tm=to).wait_send()
        send(plb.at[me], plb.at[me], pl_s.at[to], pl_r.at[me], tm=to).wait_send()
        return carry

    def sent_log(d, carry):
        to = (chip + d) % CHIPS
        send(lgt.at[chip], lgt.at[chip], lg_s.at[to], lg_r.at[chip], tm=to * 2 + core).wait_send()
        return carry

    def sent_state(to, carry):
        send(tot_s, st_t.at[chip], t_s.at[to], t_r.at[chip], tm=to * 2 + core).wait_send()
        return carry

    def sent_adjoint(to, carry):
        send(tot_a, ad_t.at[chip], a_s.at[to], a_r.at[chip], tm=to * 2 + core).wait_send()
        return carry

    lax.fori_loop(1, N_TM, sent_tm, 0)
    lax.fori_loop(1, CHIPS, sent_log, 0)
    lax.fori_loop(chip + 1, CHIPS, sent_state, 0)
    lax.fori_loop(0, chip, sent_adjoint, 0)

    gw_vm[...] = take(rs_w, rw, rw_s, rw_r)
    gw_copy = pltpu.make_async_copy(gw_vm, gw_ref, in_s.at[11])
    gw_copy.start()

    def sent_head(d, carry):
        to = (z + d) % N_HEAD
        send(rs_r.at[to], rr.at[z], rr_s.at[to], rr_r.at[z], head=to).wait_send()
        send(rs_w.at[to], rw.at[z], rw_s.at[to], rw_r.at[z], head=to).wait_send()
        return carry

    lax.fori_loop(1, N_HEAD, sent_head, 0)
    for copy in (gi_copy, gow_copy, gr_copy, gw_copy):
        copy.wait()


def write_out(gi, gw, gr, gow, gi_out, gw_out, gr_out, gow_out, gi_vm, gw_vm, gr_vm, gow_vm, came, left):
    size = gi.shape[0] // 4
    moves = [(gi.at[pl.ds(i * size, size)], gi_vm.at[pl.ds(i * size, size)], gi_out.at[pl.ds(i * size, size)]) for i in range(4)]
    moves += [(gw, gw_vm, gw_out), (gr, gr_vm, gr_out), (gow, gow_vm, gow_out)]
    ins = [pltpu.make_async_copy(a, b, came.at[i]) for i, (a, b, _) in enumerate(moves)]
    outs = [pltpu.make_async_copy(b, c, left.at[i]) for i, (_, b, c) in enumerate(moves)]
    for copy in ins:
        copy.start()
    for here, there in zip(ins, outs):
        here.wait()
        there.start()
    for copy in outs:
        copy.wait()


def body(frame_inputs, write_map, read_map, log_decay, out_weight, caption_grad, caption_start, caption_end):
    frames, width = frame_inputs.shape
    V = pltpu.VMEM
    DMA = pltpu.SemaphoreType.DMA
    state = (2, 128, 128)
    tile = (BLOCK, BLOCK)
    scratch = [
        V(frame_inputs.shape, BF16),
        V(write_map.shape, BF16),
        V(read_map.shape, BF16),
        V(log_decay.shape, F32),
        V(out_weight.shape, BF16),
        V(caption_grad.shape, F32),
        V((1, CAP), jnp.int32),
        V((1, CAP), jnp.int32),
        DMA((12,)),
        V((N_HEAD, CAP, 128), BF16),
        V((N_TM, CAP, 128), BF16),
        V((2, 8, 128), F32),
        V((2, 8, 128), F32),
        V((CAP, BLOCK), F32),
        V((CAP, BLOCK), F32),
        V((128, BLOCK), BF16),
        V((frames, 128), BF16),
        V((NH, *tile), BF16),
        V((8, frames), F32),
        V((NB, 8, BLOCK), F32),
        V((NB, *tile), F32),
        V((NB, *tile), F32),
        V((NB, 8, BLOCK), F32),
        V((NB, *tile), BF16),
        V((NB, *tile), BF16),
        V((NB, *tile), BF16),
        V((NB, 128, BLOCK), F32),
        V((NB, 128, BLOCK), F32),
        V((NB * NH, *tile), F32),
        V((NB * NH, *tile), BF16),
        V((NB, *tile), F32),
        V((NB, BLOCK, 128), F32),
        V((NB, 128, BLOCK), BF16),
        V((NB, 128, BLOCK), BF16),
        V(state, F32),
        V(state, BF16),
        V(state, BF16),
        V(state, BF16),
        V(state, F32),
        V(state, BF16),
        V((2, 8, 128), F32),
        V((2, 8, 128), F32),
        V((CHIPS, 8, 128), F32),
        V((CHIPS, 128, 128), BF16),
        V((CHIPS, 128, 128), BF16),
        V((128, 128), BF16),
        V((128, 128), BF16),
        V(state, F32),
        V(state, F32),
        V((BLOCK, 128), BF16),
        V((8, BLOCK), F32),
        V((NH, 128, 128), F32),
        V((NH, 128, 128), BF16),
        V((NH, 128, 128), BF16),
        V((BLOCK, 128), BF16),
        V((128, BLOCK), F32),
        V((CAP, BLOCK), F32),
        V((CAP, BLOCK), F32),
        V((N_TM, CAP, BLOCK), BF16),
        V((N_HEAD, 64, 128), BF16),
        V((N_HEAD, 64, 128), BF16),
        V((N_HEAD, 64, 128), BF16),
        V((N_HEAD, 64, 128), BF16),
        V((N_HEAD, 64, 128), BF16),
        V((N_HEAD, 64, 128), BF16),
        V(frame_inputs.shape, BF16),
        V((64, 128), F32),
        V((64, 128), F32),
        V((64, BLOCK), F32),
        DMA((N_HEAD,)),
        DMA((N_HEAD,)),
        DMA((N_TM,)),
        DMA((N_TM,)),
        DMA((12,)),
        DMA((12,)),
        DMA((CHIPS,)),
        DMA((CHIPS,)),
        DMA((CHIPS,)),
        DMA((CHIPS,)),
        DMA((CHIPS,)),
        DMA((CHIPS,)),
        DMA((N_TM,)),
        DMA((N_TM,)),
        DMA((N_HEAD,)),
        DMA((N_HEAD,)),
        DMA((N_HEAD,)),
        DMA((N_HEAD,)),
        DMA((N_HEAD,)),
        DMA((N_HEAD,)),
    ]
    results = pl.pallas_call(
        kernel,
        out_shape=(
            jax.ShapeDtypeStruct((frames, width), BF16),
            jax.ShapeDtypeStruct((64, 128), F32),
            jax.ShapeDtypeStruct((64, 128), F32),
            jax.ShapeDtypeStruct((64, BLOCK), F32),
        ),
        in_specs=[pl.BlockSpec(memory_space=pltpu.HBM)] * 8,
        out_specs=(pl.BlockSpec(memory_space=pltpu.HBM),) * 4,
        scratch_shapes=scratch,
        compiler_params=pltpu.CompilerParams(
            collective_id=0, has_side_effects=True, vmem_limit_bytes=63 * 1024 * 1024
        ),
    )(
        frame_inputs, write_map, read_map, log_decay, out_weight, caption_grad,
        caption_start.reshape(1, CAP), caption_end.reshape(1, CAP),
    )
    return pl.pallas_call(
        write_out,
        out_shape=tuple(jax.ShapeDtypeStruct(r.shape, r.dtype) for r in results),
        in_specs=[pl.BlockSpec(memory_space=pltpu.HBM)] * 4,
        out_specs=(pl.BlockSpec(memory_space=pltpu.HBM),) * 4,
        scratch_shapes=[V(r.shape, r.dtype) for r in results] + [DMA((7,)), DMA((7,))],
        compiler_params=pltpu.CompilerParams(vmem_limit_bytes=62 * 1024 * 1024),
    )(*results)


def solution(mesh):
    in_specs = (
        P("tm", "head"),
        P("tm", None),
        P("tm", None),
        P("head", "tm"),
        P(None, "head"),
        P("tm", "head"),
        P("tm"),
        P("tm"),
    )
    out_specs = (P("tm", "head"), P(("tm", "head"), None), P(("tm", "head"), None), P("tm", "head"))
    return jax.shard_map(body, mesh=mesh, in_specs=in_specs, out_specs=out_specs, check_vma=False)
```
